32 devices in a mesh: narrow: 4 (over x, core), wide: 8 (over z, y).
Axes of the slice: x: 2, y: 2, z: 4, core: 2. Of those that a mesh axis runs over, the one named last changes fastest.
Arguments:
- tokens: bfloat16 [64, 16384], P('narrow', 'wide'), may hold values from -6 to 6
- w_query: bfloat16 [16384, 8192], P('wide', 'narrow'), may hold values from -0.046875 to 0.046875
- w_keyval: bfloat16 [16384, 1024], P('wide', 'narrow'), may hold values from -0.046875 to 0.046875
- w_output: bfloat16 [8192, 16384], P('narrow', 'wide'), may hold values from -0.0625 to 0.0625
- grad_out: bfloat16 [64, 16384], P('narrow', 'wide'), may hold values from -6 to 6
Outputs:
- output: bfloat16 [64, 16384], P('narrow', 'wide')
- grad_tokens: bfloat16 [64, 16384], P('narrow', 'wide')
- grad_wq: bfloat16 [16384, 8192], P('wide', 'narrow')
- grad_wkv: bfloat16 [16384, 1024], P('wide', 'narrow')
- grad_wo: bfloat16 [8192, 16384], P('narrow', 'wide')
The draws below stay inside these ranges and needn't reach their ends.
All inputs are finite; a program needn't handle non-finite values.
Results may differ from the reference program's by a relative error of at most 0.015.
Values may be sent and summed in bfloat16 or wider, within the bound.
No kernel may reach another device: no remote copies, remote signals or barrier semaphores. Data moves between devices by JAX's collectives and lax.ppermute only.
A program may use at most 128 MiB of HBM per device.

```python
import jax
import jax.numpy as jnp
from jax import lax

D = 16384
H = 64
KVH = 4
HD = 128
TOKENS = 64


def shard_levels(own_key, dims, split, smallest, top_value):
    level = 1.0
    for dim, blocks in split:
        draws = jax.random.uniform(jax.random.fold_in(jax.random.fold_in(own_key, 6), dim), (blocks,), jnp.float32, smallest / len(split), top_value / len(split))
        level = level * jnp.repeat(jnp.exp(draws), dims[dim] // blocks).reshape((-1,) + (1,) * (len(dims) - 1 - dim))
    return level


def bell_draw(rng, shape, deviation, limit, split=(), dtype=jnp.bfloat16):
    factor_of = shard_levels(rng, shape, split, -0.22, 0.18) if split else 1.0
    result = jax.random.normal(rng, shape, jnp.float32) * deviation * factor_of
    return jnp.minimum(jnp.maximum(result, -limit), limit).astype(dtype)


def setup_inputs(seed: int = 0) -> dict:
    keys = jax.random.split(jax.random.key(seed), 6)
    return {
        "tokens": bell_draw(keys[0], (TOKENS, D), 1.0, 6.0, ((0, 4), (1, 8))),
        "w_query": bell_draw(keys[1], (D, H * HD), D ** -0.5, 0.046875, ((0, 8), (1, 4))),
        "w_keyval": bell_draw(keys[2], (D, 2 * KVH * HD), D ** -0.5, 0.046875, ((0, 8), (1, 4))),
        "w_output": bell_draw(keys[3], (H * HD, D), (H * HD) ** -0.5, 0.0625, ((0, 4), (1, 8))),
        "grad_out": bell_draw(keys[4], (TOKENS, D), 1.0, 6.0, ((0, 4), (1, 8))),
    }


def round_keep(value):
    return lax.optimization_barrier(value.astype(jnp.bfloat16)).astype(jnp.float32)


def reference(tokens, w_query, w_keyval, w_output, grad_out):
    group_size = H // KVH
    score_scale = HD ** -0.5
    queries = jnp.dot(tokens, w_query, preferred_element_type=jnp.float32).astype(jnp.bfloat16)
    keyval = jnp.dot(tokens, w_keyval, preferred_element_type=jnp.float32).astype(jnp.bfloat16)
    grad_att = jnp.dot(grad_out, w_output.T, preferred_element_type=jnp.float32).astype(jnp.bfloat16)
    query_groups = queries.astype(jnp.float32).reshape(TOKENS, KVH, group_size, HD).transpose(1, 2, 0, 3)
    pair_groups = keyval.astype(jnp.float32).reshape(TOKENS, KVH, 2, HD).transpose(1, 2, 0, 3)
    grad_groups = grad_att.astype(jnp.float32).reshape(TOKENS, KVH, group_size, HD).transpose(1, 2, 0, 3)
    position = jnp.arange(TOKENS)
    allowed = position[None, :] <= position[:, None]

    def one_group(inputs):
        query_group, pair_block, grad_group = inputs
        key_block = pair_block[0]
        value_block = pair_block[1]
        scores = jnp.einsum("gtd,sd->gts", query_group, key_block) * score_scale
        weights = jnp.where(allowed[None], jnp.exp(scores), 0.0)
        weights = weights / jnp.sum(weights, axis=2, keepdims=True)
        prob_bf = round_keep(weights)
        attended = jnp.einsum("gts,sd->gtd", prob_bf, value_block)
        prob_grad = jnp.einsum("gtd,sd->gts", grad_group, value_block)
        grad_values = jnp.einsum("gts,gtd->sd", prob_bf, grad_group)
        score_grad = weights * (prob_grad - jnp.sum(weights * prob_grad, axis=2, keepdims=True))
        score_half = round_keep(score_grad)
        grad_query = jnp.einsum("gts,sd->gtd", score_half, key_block) * score_scale
        grad_keys = jnp.einsum("gts,gtd->sd", score_half, query_group) * score_scale
        return attended, grad_query, jnp.stack([grad_keys, grad_values], axis=0)

    attended_all, grad_q_all, grad_pairs = lax.map(one_group, (query_groups, pair_groups, grad_groups))
    attended = attended_all.transpose(2, 0, 1, 3).reshape(TOKENS, H * HD).astype(jnp.bfloat16)
    grad_q = grad_q_all.transpose(2, 0, 1, 3).reshape(TOKENS, H * HD).astype(jnp.bfloat16)
    grad_kv = grad_pairs.transpose(2, 0, 1, 3).reshape(TOKENS, 2 * KVH * HD).astype(jnp.bfloat16)
    output = jnp.dot(attended, w_output, preferred_element_type=jnp.float32).astype(jnp.bfloat16)
    grad_wo = jnp.dot(attended.T, grad_out, preferred_element_type=jnp.float32).astype(jnp.bfloat16)
    grad_mixed = jnp.concatenate([grad_q, grad_kv], axis=1)
    grad_joined = jnp.dot(tokens.T, grad_mixed, preferred_element_type=jnp.float32)
    grad_wq = grad_joined[:, :H * HD].astype(jnp.bfloat16)
    grad_wkv = grad_joined[:, H * HD:].astype(jnp.bfloat16)
    joined = jnp.concatenate([w_query, w_keyval], axis=1)
    grad_tokens = jnp.dot(grad_mixed, joined.T, preferred_element_type=jnp.float32).astype(jnp.bfloat16)
    return (output, grad_tokens, grad_wq, grad_wkv, grad_wo)
```

```python
import functools

import jax
import jax.numpy as jnp
from jax import lax
from jax.experimental import pallas as pl
from jax.experimental.pallas import tpu as pltpu
from jax.sharding import PartitionSpec as P

HD = 128


def contract_rows(left, right):
    return lax.dot_general(
        left, right, (((0,), (0,)), ((), ())), preferred_element_type=jnp.float32
    )


def contract_cols(left, right):
    return lax.dot_general(
        left, right, (((1,), (1,)), ((), ())), preferred_element_type=jnp.float32
    )


def wide_sum(term_fn, all_rows):
    return lax.psum_scatter(
        term_fn(jnp.int32(0), lax.axis_size("wide") * (all_rows // lax.axis_size("wide"))),
        "wide",
        scatter_dimension=0,
        tiled=True,
    )


def row_shards(tokens, w_query, w_keyval, w_output, grad_out):
    wide_index = lax.axis_index("wide")
    token_panel = lax.all_gather(tokens, "narrow", axis=0, tiled=True)
    all_rows = token_panel.shape[0]
    query_cols = w_query.shape[1]
    pair_cols = w_keyval.shape[1]
    joined = jnp.concatenate([w_query, w_keyval], axis=1)

    def project_all(first_row, row_count):
        return jnp.dot(token_panel, joined, preferred_element_type=jnp.float32)

    projected = wide_sum(project_all, all_rows)
    queries = projected[:, :query_cols].astype(jnp.bfloat16)
    kv_own = projected[:, query_cols:].astype(jnp.bfloat16)
    kv_panel = lax.all_gather(kv_own, "wide", axis=0, tiled=True)
    rows_here = queries.shape[0]
    heads_here = query_cols // HD
    groups_here = pair_cols // (2 * HD)
    group_size = heads_here // groups_here
    score_scale = HD ** (-0.5)
    query_pos = wide_index * rows_here + lax.iota(jnp.int32, rows_here)
    key_pos = lax.iota(jnp.int32, all_rows)
    allowed = key_pos[None, :] <= query_pos[:, None]
    query_heads = queries.reshape(rows_here, groups_here, group_size, HD)
    pair_heads = kv_panel.reshape(all_rows, groups_here, 2, HD)
    key_heads = pair_heads[:, :, 0]
    value_heads = pair_heads[:, :, 1]
    scores = (
        jnp.einsum("rghd,sgd->ghrs", query_heads, key_heads, preferred_element_type=jnp.float32)
        * score_scale
    )
    weights = jnp.where(allowed, jnp.exp(scores), 0.0)
    weights = weights / jnp.sum(weights, axis=3, keepdims=True)
    prob_bf = weights.astype(jnp.bfloat16)
    attended = jnp.einsum(
        "ghrs,sgd->rghd", prob_bf, value_heads, preferred_element_type=jnp.float32
    )
    attended = attended.reshape(rows_here, query_cols).astype(jnp.bfloat16)
    att_panel = lax.all_gather(attended, "wide", axis=0, tiled=True)
    row_block = att_panel
    output = lax.psum_scatter(
        jnp.dot(row_block, w_output, preferred_element_type=jnp.float32).astype(jnp.bfloat16),
        "narrow",
        scatter_dimension=0,
        tiled=True,
    )
    grad_panel = lax.all_gather(grad_out, "narrow", axis=0, tiled=True)
    grad_wo = contract_rows(att_panel, grad_panel).astype(jnp.bfloat16)

    def back_out(first_row, row_count):
        return contract_cols(grad_panel, w_output)

    grad_att = wide_sum(back_out, all_rows).astype(jnp.bfloat16)
    grad_heads = grad_att.reshape(rows_here, groups_here, group_size, HD)
    prob_grad = jnp.einsum(
        "rghd,sgd->ghrs", grad_heads, value_heads, preferred_element_type=jnp.float32
    )
    grad_values = jnp.einsum(
        "ghrs,rghd->sgd", prob_bf, grad_heads, preferred_element_type=jnp.float32
    )
    score_grad = weights * (prob_grad - jnp.sum(weights * prob_grad, axis=3, keepdims=True))
    score_half = score_grad.astype(jnp.bfloat16)
    grad_q = (
        jnp.einsum("ghrs,sgd->rghd", score_half, key_heads, preferred_element_type=jnp.float32)
        * score_scale
    )
    grad_q = grad_q.reshape(rows_here, query_cols).astype(jnp.bfloat16)
    grad_keys = (
        jnp.einsum("ghrs,rghd->sgd", score_half, query_heads, preferred_element_type=jnp.float32)
        * score_scale
    )
    kv_grad = jnp.stack([grad_keys, grad_values], axis=2).reshape(all_rows, pair_cols)
    kv_share = lax.psum_scatter(kv_grad, "wide", scatter_dimension=0, tiled=True).astype(
        jnp.bfloat16
    )
    grad_mixed = jnp.concatenate([grad_q, kv_share], axis=1)
    grad_rows = lax.all_gather(grad_mixed, "wide", axis=0, tiled=True)
    grad_joined = contract_rows(token_panel, grad_rows)
    grad_wq = grad_joined[:, :query_cols].astype(jnp.bfloat16)
    grad_wkv = grad_joined[:, query_cols:].astype(jnp.bfloat16)
    row_block = grad_rows
    grad_tokens = lax.psum_scatter(
        contract_cols(row_block, joined).astype(jnp.bfloat16),
        "narrow",
        scatter_dimension=0,
        tiled=True,
    )
    return (output, grad_tokens, grad_wq, grad_wkv, grad_wo)


MIB = 1 << 20
BF = jnp.bfloat16
F32 = jnp.float32
VMEM = pl.BlockSpec(memory_space=pltpu.VMEM)
ANY = pl.BlockSpec(memory_space=pl.ANY)
HBM = pl.BlockSpec(memory_space=pltpu.HBM)


def swap(value, axis, size, distance):
    return lax.ppermute(value, axis, [(i, i ^ distance) for i in range(size)])


def call(kernel, ins, in_specs, outs, out_specs, scratch, vmem, flops, moved, aliases={}):
    return pl.pallas_call(
        kernel,
        out_shape=outs,
        in_specs=in_specs,
        out_specs=out_specs,
        scratch_shapes=scratch,
        input_output_aliases=aliases,
        compiler_params=pltpu.CompilerParams(vmem_limit_bytes=vmem),
        cost_estimate=pl.CostEstimate(flops=flops, bytes_accessed=moved, transcendentals=0),
    )(*ins)


def block_of(distance, cols):
    return pl.ds(pl.multiple_of((lax.axis_index("wide") ^ distance) * cols, cols), cols)


def load_kernel(source, wq, wo, out, sem):
    copy = pltpu.make_async_copy(source, out, sem)
    copy.start()
    copy.wait()


def panels(refs):
    half = len(refs) // 2
    return (jnp.concatenate([r[...] for r in part], axis=0) for part in (refs[:half], refs[half:]))


def query_block(wq, b, cols):
    return wq[:, block_of(b, cols)]


def output_block(wo, b, cols):
    return wo[block_of(b, cols), :]


def project_blocks(token_panel, grad_panel, blocks, wq, wo, width, out):
    cols = width // (2 * len(blocks))
    for at, b in enumerate(blocks):
        left = 2 * at * cols
        out[:, left : left + cols] = jnp.dot(token_panel, query_block(wq, b, cols), preferred_element_type=F32).astype(BF)
        out[:, left + cols : left + 2 * cols] = contract_cols(grad_panel, output_block(wo, b, cols)).astype(BF)


def project_far_kernel(blocks, count, *refs):
    pieces, (wq, wo, wkv, out, kv) = refs[:count], refs[count:]
    token_panel, grad_panel = panels(pieces)
    project_blocks(token_panel, grad_panel, blocks, wq, wo, out.shape[1], out)
    kv[...] = jnp.dot(token_panel, wkv[...], preferred_element_type=F32).astype(BF)


def project_kernel(blocks, count, *refs):
    pieces, (wq, wo, out) = refs[:count], refs[count:]
    token_panel, grad_panel = panels(pieces)
    project_blocks(token_panel, grad_panel, blocks, wq, wo, out.shape[1], out)


def last_swap_kernel(block, kv, *outs):
    cols, kv_cols = block.shape[1] // len(outs), kv.shape[1] // len(outs)
    for at, out in enumerate(outs):
        out[:, :cols] = block[:, at * cols : (at + 1) * cols]
        out[:, cols:] = kv[:, at * kv_cols : (at + 1) * kv_cols]


def add_kernel(left, right, out):
    out[...] = plus(left[...], right[...]).astype(BF)


def turn_kernel(*refs):
    refs[-1][...] = jnp.concatenate([r[...] for r in refs[:-1]], axis=0).T


def plus(left, right):
    return left.astype(F32) + right.astype(F32)


def total(parts):
    value = parts[0][...].astype(F32)
    for part in parts[1:]:
        value = value + part[...].astype(F32)
    return value


def add_far_kernel(near, far, *outs):
    width = outs[0].shape[1]
    for at, out in enumerate(outs):
        part = slice(at * width, (at + 1) * width)
        out[...] = plus(near[:, part], far[:, part]).astype(BF)


def attend_kernel(narrow, near, kv, far_query, far_grad, *refs):
    parts, out = refs[:-1], refs[-1]
    width = parts[0].shape[1]
    cols, far = width // 2, (far_query, far_grad)
    block = near[:, near.shape[1] - width :].astype(F32) + jnp.concatenate([r[:, :cols].astype(F32) for r in far], axis=1)
    block = block + total(parts)
    pair = kv[...].astype(F32) + jnp.concatenate([r[:, cols:].astype(F32) for r in far], axis=1)
    value = jnp.concatenate([block, pair], axis=1).astype(BF)
    rows = value.shape[0]
    cols = (value.shape[1] - 2 * HD) // 2
    piece = rows // narrow
    me = lax.axis_index("narrow")

    def position(dim):
        at = lax.broadcasted_iota(jnp.int32, (rows, rows), dim)
        return ((at // piece) ^ me) * piece + at % piece

    allowed = position(1) <= position(0)
    keys, values = value[:, 2 * cols : 2 * cols + HD], value[:, 2 * cols + HD :]
    scale = HD ** (-0.5)
    grad_keys = jnp.zeros((rows, HD), F32)
    grad_values = jnp.zeros((rows, HD), F32)
    for at in range(0, cols, HD):
        queries, grads = value[:, at : at + HD], value[:, cols + at : cols + at + HD]
        weights = jnp.where(allowed, jnp.exp(contract_cols(queries, keys) * scale), 0.0)
        weights = weights / jnp.sum(weights, axis=1, keepdims=True)
        probs = weights.astype(BF)
        out[:, at : at + HD] = jnp.dot(probs, values, preferred_element_type=F32).astype(BF)
        prob_grad = contract_cols(grads, values)
        score_grad = weights * (prob_grad - jnp.sum(weights * prob_grad, axis=1, keepdims=True))
        score_half = score_grad.astype(BF)
        out[:, cols + at : cols + at + HD] = (
            jnp.dot(score_half, keys, preferred_element_type=F32) * scale
        ).astype(BF)
        grad_keys = grad_keys + contract_rows(score_half, queries) * scale
        grad_values = grad_values + contract_rows(probs, grads)
    out[:, 2 * cols : 2 * cols + HD] = grad_keys.astype(BF)
    out[:, 2 * cols + HD :] = grad_values.astype(BF)


def join_kernel(width, *refs):
    parts, out = refs[:-1], refs[-1]
    kv = parts[0][:, width:].astype(F32)
    for at, part in enumerate(parts):
        out[:, at * width : (at + 1) * width] = part[:, :width]
        if at:
            kv = kv + part[:, width:].astype(F32)
    out[:, len(parts) * width :] = kv.astype(BF)


def accumulate(blocks, cols, parts, wq, wo, before, out_sum, grad_sum):
    for i, (part, left, b) in enumerate(blocks):
        out = jnp.dot(parts[part][:, left : left + cols], output_block(wo, b, cols), preferred_element_type=F32)
        grad = contract_cols(parts[part][:, left + cols : left + 2 * cols], query_block(wq, b, cols))
        if i == 0 and before:
            out, grad = out + before[0][...], grad + before[1][...]
        elif i:
            out, grad = out + out_sum[...], grad + grad_sum[...]
        out_sum[...] = out
        grad_sum[...] = grad


def back_kernel(blocks, cols, count, *refs):
    parts, (wq, wo), rest = refs[:count], refs[count : count + 2], refs[count + 2 :]
    accumulate(blocks, cols, parts, wq, wo, rest[:-2], *rest[-2:])


def kv_total(parts):
    total = parts[0][:, parts[0].shape[1] - 2 * HD :].astype(F32)
    for part in parts[1:]:
        total = total + part[:, part.shape[1] - 2 * HD :].astype(F32)
    return total.astype(BF)


def back_last_kernel(blocks, cols, count, piece, *refs):
    parts, (wq, wo, wkv, out_before, grad_before, near, far, out_sum, grad_sum) = refs[:count], refs[count:]
    accumulate(blocks, cols, parts, wq, wo, (out_before, grad_before), out_sum, grad_sum)
    grad_sum[...] += contract_cols(kv_total(parts), wkv[...])
    for out, low in ((near, 0), (far, 1)):
        for at in range(out.shape[0] // (2 * piece)):
            first = (2 * at + low) * piece
            out[2 * at * piece : (2 * at + 1) * piece, :] = out_sum[first : first + piece, :].astype(BF)
            out[(2 * at + 1) * piece : (2 * at + 2) * piece, :] = grad_sum[first : first + piece, :].astype(BF)


def send_weight_grads(blocks, cols, turned, grads, parts, gwq, gwo, gwq_v, gwo_v, sems):
    grad_panel = jnp.concatenate([r[...] for r in grads], axis=0)
    copies = []

    def send(source, target):
        copies.append(pltpu.make_async_copy(source, target, sems.at[len(copies)]))
        copies[-1].start()

    tile = 256
    for at, (part, left, b) in enumerate(blocks):
        att = parts[part][:, left : left + cols].T
        for first in range(0, gwo.shape[1], tile):
            span = slice(first, first + tile)
            gwo_v[at, :, span] = jnp.dot(att, grad_panel[:, span], preferred_element_type=F32).astype(BF)
        send(gwo_v.at[at], gwo.at[block_of(b, cols), :])
        grad = parts[part][:, left + cols : left + 2 * cols]
        for first in range(0, gwq.shape[0], tile):
            span = slice(first, first + tile)
            gwq_v[at, span, :] = jnp.dot(turned[span, :], grad, preferred_element_type=F32).astype(BF)
        send(gwq_v.at[at], gwq.at[:, block_of(b, cols)])
    return copies


def block_kernel(blocks, cols, narrow, count, has_before, *refs):
    turned, grads, parts, refs = refs[0], refs[1 : 1 + narrow], refs[1 + narrow : 1 + narrow + count], refs[1 + narrow + count :]
    wq, wo = refs[:2]
    before, outs = (refs[2:4], refs[6:]) if has_before else ((), refs[2:])
    gwq, gwo, out_sum, grad_sum, gwq_v, gwo_v, sems = outs
    copies = send_weight_grads(blocks, cols, turned, grads, parts, gwq, gwo, gwq_v, gwo_v, sems)
    accumulate(blocks, cols, parts, wq, wo, before, out_sum, grad_sum)
    for copy in copies:
        copy.wait()


def weight_grad_kernel(blocks, cols, narrow, count, *refs):
    turned, grads, parts = refs[0], refs[1 : 1 + narrow], refs[1 + narrow : 1 + narrow + count]
    gwq, gwo, gwkv, gwkv_v, gwq_v, gwo_v, sems = refs[3 + narrow + count :]
    gwkv_v[...] = jnp.dot(turned[...], kv_total(parts), preferred_element_type=F32).astype(BF)
    last = pltpu.make_async_copy(gwkv_v, gwkv, sems.at[2 * len(blocks)])
    last.start()
    copies = send_weight_grads(blocks, cols, turned, grads, parts, gwq, gwo, gwq_v, gwo_v, sems)
    for copy in copies + [last]:
        copy.wait()


def add_pieces_kernel(near, far, own, *outs):
    rows = own.shape[0]
    for at, out in enumerate((own,) + outs):
        part = slice(at * rows, (at + 1) * rows)
        out[...] = plus(near[part, :], far[part, :]).astype(BF)


def finish_kernel(*refs):
    parts, output, grad = refs[:-2], refs[-2], refs[-1]
    value = total(parts)
    rows = output.shape[0]
    output[...] = value[:rows].astype(BF)
    grad[...] = value[rows:].astype(BF)


def shards(narrow, wide, tokens, w_query, w_keyval, w_output, grad_out):
    piece, features = tokens.shape
    query_cols, pair_cols = w_query.shape[1], w_keyval.shape[1]
    cols = query_cols // wide
    if pair_cols != 2 * HD or cols % HD or cols * wide != query_cols or piece % 16 or narrow & (narrow - 1) or wide & (wide - 1) or wide < 8 or narrow < 2:
        return row_shards(tokens, w_query, w_keyval, w_output, grad_out)
    rows = narrow * piece
    weight_size = features * (2 * query_cols + pair_cols)
    full = jax.ShapeDtypeStruct((rows, 2 * cols + pair_cols), BF)
    piece_shape = jax.ShapeDtypeStruct((piece, features), BF)
    half = wide // 2
    sems = pltpu.SemaphoreType.DMA((4 * wide,))

    def spread(value):
        pieces = {0: value}
        bit = narrow // 2
        while bit > 1:
            pieces.update({b ^ bit: swap(p, "narrow", narrow, bit) for b, p in pieces.items()})
            bit //= 2
        return {b: p for b, p in pieces.items() if b}

    token_pieces, grad_pieces = spread(tokens), spread(grad_out)
    beside = [{0: v, 1: swap(v, "narrow", narrow, 1)} for v in (tokens, grad_out)]
    far_blocks = list(range(wide - 1, 0, -2))
    near_blocks = list(range(wide - 2, -1, -2))
    wkv = call(
        load_kernel,
        [pltpu.with_memory_space_constraint(w, pltpu.HBM) for w in (w_keyval, w_query, w_output)],
        [HBM] * 3,
        jax.ShapeDtypeStruct(w_keyval.shape, BF),
        VMEM,
        [pltpu.SemaphoreType.DMA],
        2 * MIB,
        0,
        2 * weight_size,
    )
    token_pieces, grad_pieces, wkv = lax.optimization_barrier((token_pieces, grad_pieces, wkv))
    for pieces in (token_pieces, grad_pieces):
        pieces.update({b ^ 1: swap(p, "narrow", narrow, 1) for b, p in pieces.items() if b})
    token_pieces, grad_pieces = [[{**own, **p}[b] for b in range(narrow)] for own, p in zip(beside, (token_pieces, grad_pieces))]
    most = half - 1
    pieces = (*token_pieces, *grad_pieces)
    count = 2 * narrow
    far, kv = call(
        functools.partial(project_far_kernel, far_blocks[:most], count),
        (*pieces, w_query, w_output, wkv),
        [VMEM] * (count + 3),
        [
            jax.ShapeDtypeStruct((rows, 2 * cols * most), BF),
            jax.ShapeDtypeStruct((rows, pair_cols), BF),
        ],
        [VMEM] * 2,
        [],
        8 * MIB,
        rows * weight_size,
        weight_size,
    )
    far = swap(far, "wide", wide, 1)
    def project(blocks):
        return call(
            functools.partial(project_kernel, blocks, count),
            (*pieces, w_query, w_output),
            [VMEM] * (count + 2),
            jax.ShapeDtypeStruct((rows, 2 * cols * len(blocks)), BF),
            VMEM,
            [],
            8 * MIB,
            2 * rows * weight_size * len(blocks) // wide,
            2 * weight_size * len(blocks) // wide,
        )

    near = project(near_blocks)
    bit = 2
    while bit < wide:
        other = swap(kv, "wide", wide, bit)
        if bit == 2:
            other, near = lax.optimization_barrier((other, near))
        kv = call(
            add_kernel,
            (kv, other),
            [VMEM] * 2,
            jax.ShapeDtypeStruct((rows, pair_cols), BF),
            VMEM,
            [],
            2 * MIB,
            2 * rows * pair_cols,
            6 * rows * pair_cols,
        )
        bit *= 2
    turned = call(
        turn_kernel,
        token_pieces,
        [VMEM] * narrow,
        jax.ShapeDtypeStruct((features, rows), BF),
        VMEM,
        [],
        2 * MIB,
        0,
        4 * rows * features,
    )
    near, turned = lax.optimization_barrier((near, turned))
    sums = call(
        add_far_kernel,
        (near, far),
        [VMEM] * 2,
        [jax.ShapeDtypeStruct((rows, 2 * cols), BF)] * most,
        [VMEM] * most,
        [],
        2 * MIB,
        rows * 2048,
        rows * 8192,
    )
    received = [swap(part, "wide", wide, d) for part, d in zip(sums, near_blocks)][::-1]
    far_own = call(
        last_swap_kernel,
        (project(far_blocks[most:]), kv),
        [VMEM] * 2,
        [jax.ShapeDtypeStruct((rows, cols + HD), BF)] * 2,
        [VMEM] * 2,
        [],
        2 * MIB,
        0,
        4 * rows * full.shape[1],
    )
    far_other = [swap(part, "wide", wide, 1) for part in far_own]
    own = call(
        functools.partial(attend_kernel, narrow),
        (near, kv, *far_other, *received),
        [VMEM] * (4 + len(received)),
        full,
        VMEM,
        [],
        4 * MIB,
        24 * rows * rows * cols,
        2 * rows * wide * full.shape[1],
    )
    width = 2 * cols
    same = {0: own, **{d: swap(own, "wide", wide, d) for d in near_blocks[:-1]}}
    width = 2 * cols
    sum_shapes = [jax.ShapeDtypeStruct((rows, features), F32)] * 2
    grad_shapes = [jax.ShapeDtypeStruct(w.shape, BF) for w in (w_query, w_output)]

    def grad_scratch(blocks):
        return [pltpu.VMEM((len(blocks), features, cols), BF), pltpu.VMEM((len(blocks), cols, features), BF), sems]

    def block_terms(distances, before=()):
        blocks = [(i, 0, d) for i, d in enumerate(distances)]
        ins = (turned, *grad_pieces, *[same[d] for d in distances], w_query, w_output, *before)
        return call(
            functools.partial(block_kernel, blocks, cols, narrow, len(blocks), bool(before)),
            ins,
            [VMEM] * (3 + narrow + len(blocks)) + ([VMEM] * 2 + [ANY] * 2 if before else []),
            grad_shapes + sum_shapes,
            [ANY] * 2 + [VMEM] * 2,
            grad_scratch(blocks),
            20 * MIB,
            8 * rows * features * cols * len(blocks),
            8 * features * cols * len(blocks),
            {len(ins) - 2: 0, len(ins) - 1: 1} if before else {},
        )

    same = {0: own, **{d: swap(own, "wide", wide, d) for d in near_blocks[:-1]}}
    first, rest = near_blocks[-2], near_blocks[:-2]
    groups = ([0, first], rest)
    joined = []
    for group in groups:
        if joined:
            *grads, out_sum, grad_sum = block_terms([0, first])
            same[rest[-1]], grads, out_sum, grad_sum = lax.optimization_barrier((same[rest[-1]], grads, out_sum, grad_sum))
        together = call(
            functools.partial(join_kernel, width),
            [same[d] for d in group],
            [VMEM] * len(group),
            jax.ShapeDtypeStruct((rows, width * len(group) + pair_cols), BF),
            VMEM,
            [],
            2 * MIB,
            0,
            4 * rows * full.shape[1] * len(group),
        )
        joined.append(swap(together, "wide", wide, 1))
    *grads, out_sum, grad_sum = block_terms(rest, (out_sum, grad_sum, *grads))
    blocks = [[(i, width * at, d + 1) for at, d in enumerate(group)] for i, group in enumerate(groups)]
    out_sum, grad_sum = call(
        functools.partial(back_kernel, blocks[0], cols, 1),
        (joined[0], w_query, w_output, out_sum, grad_sum),
        [VMEM] * 5,
        sum_shapes,
        [VMEM] * 2,
        [],
        8 * MIB,
        4 * rows * features * cols * len(blocks[0]),
        4 * features * cols * len(blocks[0]),
    )
    parts = [*joined, *same.values()]
    piece_half = jax.ShapeDtypeStruct((narrow * piece, features), BF)
    piece_pair = jax.ShapeDtypeStruct((2 * piece, features), BF)
    near, far = call(
        functools.partial(back_last_kernel, blocks[1], cols, len(parts), piece),
        (*parts, w_query, w_output, wkv, out_sum, grad_sum),
        [VMEM] * (len(parts) + 5),
        [piece_half] * 2,
        [VMEM] * 2,
        [pltpu.VMEM((rows, features), F32), pltpu.VMEM((rows, features), F32)],
        8 * MIB,
        rows * weight_size,
        weight_size,
    )
    far = swap(far, "narrow", narrow, 1)
    sums = call(
        add_pieces_kernel,
        (near, far),
        [VMEM] * 2,
        [piece_pair] * (narrow // 2),
        [VMEM] * (narrow // 2),
        [],
        2 * MIB,
        2 * rows * features,
        12 * rows * features,
    )
    sums = [sums[0]] + [swap(sums[i], "narrow", narrow, 2 * i) for i in range(1, narrow // 2)]
    blocks = blocks[0] + blocks[1]
    ins = (turned, *grad_pieces, *parts, *grads)
    grad_wq, grad_wo, grad_wkv = call(
        functools.partial(weight_grad_kernel, blocks, cols, narrow, len(parts)),
        ins,
        [VMEM] * (1 + narrow + len(parts)) + [ANY] * 2,
        grad_shapes + [jax.ShapeDtypeStruct(w_keyval.shape, BF)],
        [ANY] * 3,
        [pltpu.VMEM(w_keyval.shape, BF)] + grad_scratch(blocks),
        20 * MIB,
        8 * rows * features * cols * len(blocks),
        8 * features * cols * len(blocks),
        {len(ins) - 2: 0, len(ins) - 1: 1},
    )
    output, grad_tokens = call(
        finish_kernel,
        sums,
        [VMEM] * len(sums),
        [piece_shape] * 2,
        [VMEM] * 2,
        [],
        4 * MIB,
        2 * narrow * piece * features,
        4 * narrow * piece * features,
    )
    return (output, grad_tokens, grad_wq, grad_wkv, grad_wo)


def solution(mesh):
    return jax.shard_map(
        functools.partial(shards, mesh.shape["narrow"], mesh.shape["wide"]),
        mesh=mesh,
        in_specs=(
            P("narrow", "wide"),
            P("wide", "narrow"),
            P("wide", "narrow"),
            P("narrow", "wide"),
            P("narrow", "wide"),
        ),
        out_specs=(
            P("narrow", "wide"),
            P("narrow", "wide"),
            P("wide", "narrow"),
            P("wide", "narrow"),
            P("narrow", "wide"),
        ),
        check_vma=False,
    )
```

```python
import functools

import jax
import jax.numpy as jnp
from jax import lax
from jax.experimental import pallas as pl
from jax.experimental.pallas import tpu as pltpu
from jax.sharding import PartitionSpec as P

HD = 128


def contract_rows(left, right):
    return lax.dot_general(
        left, right, (((0,), (0,)), ((), ())), preferred_element_type=jnp.float32
    )


def contract_cols(left, right):
    return lax.dot_general(
        left, right, (((1,), (1,)), ((), ())), preferred_element_type=jnp.float32
    )


def wide_sum(term_fn, all_rows):
    return lax.psum_scatter(
        term_fn(jnp.int32(0), lax.axis_size("wide") * (all_rows // lax.axis_size("wide"))),
        "wide",
        scatter_dimension=0,
        tiled=True,
    )


def row_shards(tokens, w_query, w_keyval, w_output, grad_out):
    wide_index = lax.axis_index("wide")
    token_panel = lax.all_gather(tokens, "narrow", axis=0, tiled=True)
    all_rows = token_panel.shape[0]
    query_cols = w_query.shape[1]
    pair_cols = w_keyval.shape[1]
    joined = jnp.concatenate([w_query, w_keyval], axis=1)

    def project_all(first_row, row_count):
        return jnp.dot(token_panel, joined, preferred_element_type=jnp.float32)

    projected = wide_sum(project_all, all_rows)
    queries = projected[:, :query_cols].astype(jnp.bfloat16)
    kv_own = projected[:, query_cols:].astype(jnp.bfloat16)
    kv_panel = lax.all_gather(kv_own, "wide", axis=0, tiled=True)
    rows_here = queries.shape[0]
    heads_here = query_cols // HD
    groups_here = pair_cols // (2 * HD)
    group_size = heads_here // groups_here
    score_scale = HD ** (-0.5)
    query_pos = wide_index * rows_here + lax.iota(jnp.int32, rows_here)
    key_pos = lax.iota(jnp.int32, all_rows)
    allowed = key_pos[None, :] <= query_pos[:, None]
    query_heads = queries.reshape(rows_here, groups_here, group_size, HD)
    pair_heads = kv_panel.reshape(all_rows, groups_here, 2, HD)
    key_heads = pair_heads[:, :, 0]
    value_heads = pair_heads[:, :, 1]
    scores = (
        jnp.einsum("rghd,sgd->ghrs", query_heads, key_heads, preferred_element_type=jnp.float32)
        * score_scale
    )
    weights = jnp.where(allowed, jnp.exp(scores), 0.0)
    weights = weights / jnp.sum(weights, axis=3, keepdims=True)
    prob_bf = weights.astype(jnp.bfloat16)
    attended = jnp.einsum(
        "ghrs,sgd->rghd", prob_bf, value_heads, preferred_element_type=jnp.float32
    )
    attended = attended.reshape(rows_here, query_cols).astype(jnp.bfloat16)
    att_panel = lax.all_gather(attended, "wide", axis=0, tiled=True)
    row_block = att_panel
    output = lax.psum_scatter(
        jnp.dot(row_block, w_output, preferred_element_type=jnp.float32).astype(jnp.bfloat16),
        "narrow",
        scatter_dimension=0,
        tiled=True,
    )
    grad_panel = lax.all_gather(grad_out, "narrow", axis=0, tiled=True)
    grad_wo = contract_rows(att_panel, grad_panel).astype(jnp.bfloat16)

    def back_out(first_row, row_count):
        return contract_cols(grad_panel, w_output)

    grad_att = wide_sum(back_out, all_rows).astype(jnp.bfloat16)
    grad_heads = grad_att.reshape(rows_here, groups_here, group_size, HD)
    prob_grad = jnp.einsum(
        "rghd,sgd->ghrs", grad_heads, value_heads, preferred_element_type=jnp.float32
    )
    grad_values = jnp.einsum(
        "ghrs,rghd->sgd", prob_bf, grad_heads, preferred_element_type=jnp.float32
    )
    score_grad = weights * (prob_grad - jnp.sum(weights * prob_grad, axis=3, keepdims=True))
    score_half = score_grad.astype(jnp.bfloat16)
    grad_q = (
        jnp.einsum("ghrs,sgd->rghd", score_half, key_heads, preferred_element_type=jnp.float32)
        * score_scale
    )
    grad_q = grad_q.reshape(rows_here, query_cols).astype(jnp.bfloat16)
    grad_keys = (
        jnp.einsum("ghrs,rghd->sgd", score_half, query_heads, preferred_element_type=jnp.float32)
        * score_scale
    )
    kv_grad = jnp.stack([grad_keys, grad_values], axis=2).reshape(all_rows, pair_cols)
    kv_share = lax.psum_scatter(kv_grad, "wide", scatter_dimension=0, tiled=True).astype(
        jnp.bfloat16
    )
    grad_mixed = jnp.concatenate([grad_q, kv_share], axis=1)
    grad_rows = lax.all_gather(grad_mixed, "wide", axis=0, tiled=True)
    grad_joined = contract_rows(token_panel, grad_rows)
    grad_wq = grad_joined[:, :query_cols].astype(jnp.bfloat16)
    grad_wkv = grad_joined[:, query_cols:].astype(jnp.bfloat16)
    row_block = grad_rows
    grad_tokens = lax.psum_scatter(
        contract_cols(row_block, joined).astype(jnp.bfloat16),
        "narrow",
        scatter_dimension=0,
        tiled=True,
    )
    return (output, grad_tokens, grad_wq, grad_wkv, grad_wo)


MIB = 1 << 20
BF = jnp.bfloat16
F32 = jnp.float32
VMEM = pl.BlockSpec(memory_space=pltpu.VMEM)
ANY = pl.BlockSpec(memory_space=pl.ANY)
HBM = pl.BlockSpec(memory_space=pltpu.HBM)


def swap(value, axis, size, distance):
    return lax.ppermute(value, axis, [(i, i ^ distance) for i in range(size)])


def call(kernel, ins, in_specs, outs, out_specs, scratch, vmem, flops, moved, aliases={}):
    return pl.pallas_call(
        kernel,
        out_shape=outs,
        in_specs=in_specs,
        out_specs=out_specs,
        scratch_shapes=scratch,
        input_output_aliases=aliases,
        compiler_params=pltpu.CompilerParams(vmem_limit_bytes=vmem),
        cost_estimate=pl.CostEstimate(flops=flops, bytes_accessed=moved, transcendentals=0),
    )(*ins)


def block_of(distance, cols):
    return pl.ds(pl.multiple_of((lax.axis_index("wide") ^ distance) * cols, cols), cols)


def load_kernel(source, wq, wo, out, sem):
    copy = pltpu.make_async_copy(source, out, sem)
    copy.start()
    copy.wait()


def panels(refs):
    half = len(refs) // 2
    return (jnp.concatenate([r[...] for r in part], axis=0) for part in (refs[:half], refs[half:]))


def query_block(wq, b, cols):
    return wq[:, block_of(b, cols)]


def output_block(wo, b, cols):
    return wo[block_of(b, cols), :]


def project_blocks(token_panel, grad_panel, blocks, wq, wo, width, out):
    cols = width // (2 * len(blocks))
    for at, b in enumerate(blocks):
        left = 2 * at * cols
        out[:, left : left + cols] = jnp.dot(token_panel, query_block(wq, b, cols), preferred_element_type=F32).astype(BF)
        out[:, left + cols : left + 2 * cols] = contract_cols(grad_panel, output_block(wo, b, cols)).astype(BF)


def project_far_kernel(blocks, count, *refs):
    pieces, (wq, wo, wkv, out, kv) = refs[:count], refs[count:]
    token_panel, grad_panel = panels(pieces)
    project_blocks(token_panel, grad_panel, blocks, wq, wo, out.shape[1], out)
    kv[...] = jnp.dot(token_panel, wkv[...], preferred_element_type=F32).astype(BF)


def project_kernel(blocks, count, *refs):
    pieces, (wq, wo, out) = refs[:count], refs[count:]
    token_panel, grad_panel = panels(pieces)
    project_blocks(token_panel, grad_panel, blocks, wq, wo, out.shape[1], out)


def last_swap_kernel(block, kv, *outs):
    cols, kv_cols = block.shape[1] // len(outs), kv.shape[1] // len(outs)
    for at, out in enumerate(outs):
        out[:, :cols] = block[:, at * cols : (at + 1) * cols]
        out[:, cols:] = kv[:, at * kv_cols : (at + 1) * kv_cols]


def add_kernel(left, right, out):
    out[...] = plus(left[...], right[...]).astype(BF)


def turn_kernel(*refs):
    refs[-1][...] = jnp.concatenate([r[...] for r in refs[:-1]], axis=0).T


def plus(left, right):
    return left.astype(F32) + right.astype(F32)


def total(parts):
    value = parts[0][...].astype(F32)
    for part in parts[1:]:
        value = value + part[...].astype(F32)
    return value


def add_far_kernel(near, far, *outs):
    width = outs[0].shape[1]
    for at, out in enumerate(outs):
        part = slice(at * width, (at + 1) * width)
        out[...] = plus(near[:, part], far[:, part]).astype(BF)


def attend_kernel(narrow, near, kv, far_query, far_grad, *refs):
    parts, out = refs[:-1], refs[-1]
    width = parts[0].shape[1]
    cols, far = width // 2, (far_query, far_grad)
    block = near[...].astype(F32) + jnp.concatenate([r[:, :cols].astype(F32) for r in far], axis=1)
    block = block + total(parts)
    pair = kv[...].astype(F32) + jnp.concatenate([r[:, cols:].astype(F32) for r in far], axis=1)
    value = jnp.concatenate([block, pair], axis=1).astype(BF)
    rows = value.shape[0]
    cols = (value.shape[1] - 2 * HD) // 2
    piece = rows // narrow
    me = lax.axis_index("narrow")

    def position(dim):
        at = lax.broadcasted_iota(jnp.int32, (rows, rows), dim)
        return ((at // piece) ^ me) * piece + at % piece

    allowed = position(1) <= position(0)
    keys, values = value[:, 2 * cols : 2 * cols + HD], value[:, 2 * cols + HD :]
    scale = HD ** (-0.5)
    grad_keys = jnp.zeros((rows, HD), F32)
    grad_values = jnp.zeros((rows, HD), F32)
    for at in range(0, cols, HD):
        queries, grads = value[:, at : at + HD], value[:, cols + at : cols + at + HD]
        weights = jnp.where(allowed, jnp.exp(contract_cols(queries, keys) * scale), 0.0)
        weights = weights / jnp.sum(weights, axis=1, keepdims=True)
        probs = weights.astype(BF)
        out[:, at : at + HD] = jnp.dot(probs, values, preferred_element_type=F32).astype(BF)
        prob_grad = contract_cols(grads, values)
        score_grad = weights * (prob_grad - jnp.sum(weights * prob_grad, axis=1, keepdims=True))
        score_half = score_grad.astype(BF)
        out[:, cols + at : cols + at + HD] = (
            jnp.dot(score_half, keys, preferred_element_type=F32) * scale
        ).astype(BF)
        grad_keys = grad_keys + contract_rows(score_half, queries) * scale
        grad_values = grad_values + contract_rows(probs, grads)
    out[:, 2 * cols : 2 * cols + HD] = grad_keys.astype(BF)
    out[:, 2 * cols + HD :] = grad_values.astype(BF)


def join_kernel(width, *refs):
    parts, out = refs[:-1], refs[-1]
    kv = parts[0][:, width:].astype(F32)
    for at, part in enumerate(parts):
        out[:, at * width : (at + 1) * width] = part[:, :width]
        if at:
            kv = kv + part[:, width:].astype(F32)
    out[:, len(parts) * width :] = kv.astype(BF)


def accumulate(blocks, cols, parts, wq, wo, before, out_sum, grad_sum):
    for i, (part, left, b) in enumerate(blocks):
        out = jnp.dot(parts[part][:, left : left + cols], output_block(wo, b, cols), preferred_element_type=F32)
        grad = contract_cols(parts[part][:, left + cols : left + 2 * cols], query_block(wq, b, cols))
        if i == 0 and before:
            out, grad = out + before[0][...], grad + before[1][...]
        elif i:
            out, grad = out + out_sum[...], grad + grad_sum[...]
        out_sum[...] = out
        grad_sum[...] = grad


def back_kernel(blocks, cols, count, *refs):
    parts, (wq, wo), rest = refs[:count], refs[count : count + 2], refs[count + 2 :]
    accumulate(blocks, cols, parts, wq, wo, rest[:-2], *rest[-2:])


def kv_total(parts):
    total = parts[0][:, parts[0].shape[1] - 2 * HD :].astype(F32)
    for part in parts[1:]:
        total = total + part[:, part.shape[1] - 2 * HD :].astype(F32)
    return total.astype(BF)


def back_last_kernel(blocks, cols, count, piece, *refs):
    parts, (wq, wo, wkv, out_before, grad_before, near, far, out_sum, grad_sum) = refs[:count], refs[count:]
    accumulate(blocks, cols, parts, wq, wo, (out_before, grad_before), out_sum, grad_sum)
    grad_sum[...] += contract_cols(kv_total(parts), wkv[...])
    for out, low in ((near, 0), (far, 1)):
        for at in range(out.shape[0] // (2 * piece)):
            first = (2 * at + low) * piece
            out[2 * at * piece : (2 * at + 1) * piece, :] = out_sum[first : first + piece, :].astype(BF)
            out[(2 * at + 1) * piece : (2 * at + 2) * piece, :] = grad_sum[first : first + piece, :].astype(BF)


def send_weight_grads(blocks, cols, turned, grads, parts, gwq, gwo, gwq_v, gwo_v, sems):
    grad_panel = jnp.concatenate([r[...] for r in grads], axis=0)
    copies = []

    def send(source, target):
        copies.append(pltpu.make_async_copy(source, target, sems.at[len(copies)]))
        copies[-1].start()

    tile = 256
    for at, (part, left, b) in enumerate(blocks):
        att = parts[part][:, left : left + cols].T
        for first in range(0, gwo.shape[1], tile):
            span = slice(first, first + tile)
            gwo_v[at, :, span] = jnp.dot(att, grad_panel[:, span], preferred_element_type=F32).astype(BF)
        send(gwo_v.at[at], gwo.at[block_of(b, cols), :])
        grad = parts[part][:, left + cols : left + 2 * cols]
        for first in range(0, gwq.shape[0], tile):
            span = slice(first, first + tile)
            gwq_v[at, span, :] = jnp.dot(turned[span, :], grad, preferred_element_type=F32).astype(BF)
        send(gwq_v.at[at], gwq.at[:, block_of(b, cols)])
    return copies


def block_kernel(blocks, cols, narrow, count, has_before, *refs):
    turned, grads, parts, refs = refs[0], refs[1 : 1 + narrow], refs[1 + narrow : 1 + narrow + count], refs[1 + narrow + count :]
    wq, wo = refs[:2]
    before, outs = (refs[2:4], refs[6:]) if has_before else ((), refs[2:])
    gwq, gwo, out_sum, grad_sum, gwq_v, gwo_v, sems = outs
    copies = send_weight_grads(blocks, cols, turned, grads, parts, gwq, gwo, gwq_v, gwo_v, sems)
    accumulate(blocks, cols, parts, wq, wo, before, out_sum, grad_sum)
    for copy in copies:
        copy.wait()


def weight_grad_kernel(blocks, cols, narrow, count, *refs):
    turned, grads, parts = refs[0], refs[1 : 1 + narrow], refs[1 + narrow : 1 + narrow + count]
    gwq, gwo, gwkv, gwkv_v, gwq_v, gwo_v, sems = refs[3 + narrow + count :]
    gwkv_v[...] = jnp.dot(turned[...], kv_total(parts), preferred_element_type=F32).astype(BF)
    last = pltpu.make_async_copy(gwkv_v, gwkv, sems.at[2 * len(blocks)])
    last.start()
    copies = send_weight_grads(blocks, cols, turned, grads, parts, gwq, gwo, gwq_v, gwo_v, sems)
    for copy in copies + [last]:
        copy.wait()


def add_pieces_kernel(near, far, own, *outs):
    rows = own.shape[0]
    for at, out in enumerate((own,) + outs):
        part = slice(at * rows, (at + 1) * rows)
        out[...] = plus(near[part, :], far[part, :]).astype(BF)


def finish_kernel(*refs):
    parts, output, grad = refs[:-2], refs[-2], refs[-1]
    value = total(parts)
    rows = output.shape[0]
    output[...] = value[:rows].astype(BF)
    grad[...] = value[rows:].astype(BF)


def shards(narrow, wide, tokens, w_query, w_keyval, w_output, grad_out):
    piece, features = tokens.shape
    query_cols, pair_cols = w_query.shape[1], w_keyval.shape[1]
    cols = query_cols // wide
    if pair_cols != 2 * HD or cols % HD or cols * wide != query_cols or piece % 16 or narrow & (narrow - 1) or wide & (wide - 1) or wide < 8 or narrow < 2:
        return row_shards(tokens, w_query, w_keyval, w_output, grad_out)
    rows = narrow * piece
    weight_size = features * (2 * query_cols + pair_cols)
    full = jax.ShapeDtypeStruct((rows, 2 * cols + pair_cols), BF)
    piece_shape = jax.ShapeDtypeStruct((piece, features), BF)
    half = wide // 2
    sems = pltpu.SemaphoreType.DMA((4 * wide,))

    def spread(value):
        pieces = {0: value}
        bit = narrow // 2
        while bit > 1:
            pieces.update({b ^ bit: swap(p, "narrow", narrow, bit) for b, p in pieces.items()})
            bit //= 2
        return {b: p for b, p in pieces.items() if b}

    token_pieces, grad_pieces = spread(tokens), spread(grad_out)
    beside = [{0: v, 1: swap(v, "narrow", narrow, 1)} for v in (tokens, grad_out)]
    far_blocks = list(range(wide - 1, 0, -2))
    near_blocks = list(range(wide - 2, -1, -2))
    wkv = call(
        load_kernel,
        [pltpu.with_memory_space_constraint(w, pltpu.HBM) for w in (w_keyval, w_query, w_output)],
        [HBM] * 3,
        jax.ShapeDtypeStruct(w_keyval.shape, BF),
        VMEM,
        [pltpu.SemaphoreType.DMA],
        2 * MIB,
        0,
        2 * weight_size,
    )
    token_pieces, grad_pieces, wkv = lax.optimization_barrier((token_pieces, grad_pieces, wkv))
    for pieces in (token_pieces, grad_pieces):
        pieces.update({b ^ 1: swap(p, "narrow", narrow, 1) for b, p in pieces.items() if b})
    token_pieces, grad_pieces = [[{**own, **p}[b] for b in range(narrow)] for own, p in zip(beside, (token_pieces, grad_pieces))]
    most = half - 1
    pieces = (*token_pieces, *grad_pieces)
    count = 2 * narrow
    far, kv = call(
        functools.partial(project_far_kernel, far_blocks[:most], count),
        (*pieces, w_query, w_output, wkv),
        [VMEM] * (count + 3),
        [
            jax.ShapeDtypeStruct((rows, 2 * cols * most), BF),
            jax.ShapeDtypeStruct((rows, pair_cols), BF),
        ],
        [VMEM] * 2,
        [],
        8 * MIB,
        rows * weight_size,
        weight_size,
    )
    far = swap(far, "wide", wide, 1)
    def project(blocks, pieces=pieces):
        return call(
            functools.partial(project_kernel, blocks, count),
            (*pieces, w_query, w_output),
            [VMEM] * (count + 2),
            jax.ShapeDtypeStruct((rows, 2 * cols * len(blocks)), BF),
            VMEM,
            [],
            8 * MIB,
            2 * rows * weight_size * len(blocks) // wide,
            2 * weight_size * len(blocks) // wide,
        )

    near = project(near_blocks[:-1])
    bit = 2
    while bit < wide:
        other = swap(kv, "wide", wide, bit)
        if bit == 2:
            other, _ = lax.optimization_barrier((other, near))
        kv = call(
            add_kernel,
            (kv, other),
            [VMEM] * 2,
            jax.ShapeDtypeStruct((rows, pair_cols), BF),
            VMEM,
            [],
            2 * MIB,
            2 * rows * pair_cols,
            6 * rows * pair_cols,
        )
        bit *= 2
    sums = call(
        add_far_kernel,
        (near, far),
        [VMEM] * 2,
        [jax.ShapeDtypeStruct((rows, 2 * cols), BF)] * most,
        [VMEM] * most,
        [],
        2 * MIB,
        rows * 2048,
        rows * 8192,
    )
    received = [swap(part, "wide", wide, d) for part, d in zip(sums, near_blocks)]
    later, _ = lax.optimization_barrier((pieces, sums[-1]))
    near_last = project(near_blocks[-1:], later)
    turned = call(
        turn_kernel,
        later[:narrow],
        [VMEM] * narrow,
        jax.ShapeDtypeStruct((features, rows), BF),
        VMEM,
        [],
        2 * MIB,
        0,
        4 * rows * features,
    )
    near_last, turned = lax.optimization_barrier((near_last, turned))
    far_own = call(
        last_swap_kernel,
        (project(far_blocks[most:]), kv),
        [VMEM] * 2,
        [jax.ShapeDtypeStruct((rows, cols + HD), BF)] * 2,
        [VMEM] * 2,
        [],
        2 * MIB,
        0,
        4 * rows * full.shape[1],
    )
    far_other = [swap(part, "wide", wide, 1) for part in far_own]
    own = call(
        functools.partial(attend_kernel, narrow),
        (near_last, kv, *far_other, *received),
        [VMEM] * (4 + len(received)),
        full,
        VMEM,
        [],
        4 * MIB,
        24 * rows * rows * cols,
        2 * rows * wide * full.shape[1],
    )
    width = 2 * cols
    same = {0: own, **{d: swap(own, "wide", wide, d) for d in near_blocks[:-1]}}
    width = 2 * cols
    sum_shapes = [jax.ShapeDtypeStruct((rows, features), F32)] * 2
    grad_shapes = [jax.ShapeDtypeStruct(w.shape, BF) for w in (w_query, w_output)]

    def grad_scratch(blocks):
        return [pltpu.VMEM((len(blocks), features, cols), BF), pltpu.VMEM((len(blocks), cols, features), BF), sems]

    def block_terms(distances, before=()):
        blocks = [(i, 0, d) for i, d in enumerate(distances)]
        ins = (turned, *grad_pieces, *[same[d] for d in distances], w_query, w_output, *before)
        return call(
            functools.partial(block_kernel, blocks, cols, narrow, len(blocks), bool(before)),
            ins,
            [VMEM] * (3 + narrow + len(blocks)) + ([VMEM] * 2 + [ANY] * 2 if before else []),
            grad_shapes + sum_shapes,
            [ANY] * 2 + [VMEM] * 2,
            grad_scratch(blocks),
            20 * MIB,
            8 * rows * features * cols * len(blocks),
            8 * features * cols * len(blocks),
            {len(ins) - 2: 0, len(ins) - 1: 1} if before else {},
        )

    same = {0: own, **{d: swap(own, "wide", wide, d) for d in near_blocks[:-1]}}
    first, rest = near_blocks[-2], near_blocks[:-2]
    groups = ([0, first], rest)
    joined = []
    for group in groups:
        if joined:
            *grads, out_sum, grad_sum = block_terms([0, first])
            same[rest[-1]], grads, out_sum, grad_sum = lax.optimization_barrier((same[rest[-1]], grads, out_sum, grad_sum))
        together = call(
            functools.partial(join_kernel, width),
            [same[d] for d in group],
            [VMEM] * len(group),
            jax.ShapeDtypeStruct((rows, width * len(group) + pair_cols), BF),
            VMEM,
            [],
            2 * MIB,
            0,
            4 * rows * full.shape[1] * len(group),
        )
        joined.append(swap(together, "wide", wide, 1))
    *grads, out_sum, grad_sum = block_terms(rest, (out_sum, grad_sum, *grads))
    blocks = [[(i, width * at, d + 1) for at, d in enumerate(group)] for i, group in enumerate(groups)]
    out_sum, grad_sum = call(
        functools.partial(back_kernel, blocks[0], cols, 1),
        (joined[0], w_query, w_output, out_sum, grad_sum),
        [VMEM] * 5,
        sum_shapes,
        [VMEM] * 2,
        [],
        8 * MIB,
        4 * rows * features * cols * len(blocks[0]),
        4 * features * cols * len(blocks[0]),
    )
    parts = [*joined, *same.values()]
    piece_half = jax.ShapeDtypeStruct((narrow * piece, features), BF)
    piece_pair = jax.ShapeDtypeStruct((2 * piece, features), BF)
    near, far = call(
        functools.partial(back_last_kernel, blocks[1], cols, len(parts), piece),
        (*parts, w_query, w_output, wkv, out_sum, grad_sum),
        [VMEM] * (len(parts) + 5),
        [piece_half] * 2,
        [VMEM] * 2,
        [pltpu.VMEM((rows, features), F32), pltpu.VMEM((rows, features), F32)],
        8 * MIB,
        rows * weight_size,
        weight_size,
    )
    far = swap(far, "narrow", narrow, 1)
    sums = call(
        add_pieces_kernel,
        (near, far),
        [VMEM] * 2,
        [piece_pair] * (narrow // 2),
        [VMEM] * (narrow // 2),
        [],
        2 * MIB,
        2 * rows * features,
        12 * rows * features,
    )
    sums = [sums[0]] + [swap(sums[i], "narrow", narrow, 2 * i) for i in range(1, narrow // 2)]
    blocks = blocks[0] + blocks[1]
    ins = (turned, *grad_pieces, *parts, *grads)
    grad_wq, grad_wo, grad_wkv = call(
        functools.partial(weight_grad_kernel, blocks, cols, narrow, len(parts)),
        ins,
        [VMEM] * (1 + narrow + len(parts)) + [ANY] * 2,
        grad_shapes + [jax.ShapeDtypeStruct(w_keyval.shape, BF)],
        [ANY] * 3,
        [pltpu.VMEM(w_keyval.shape, BF)] + grad_scratch(blocks),
        20 * MIB,
        8 * rows * features * cols * len(blocks),
        8 * features * cols * len(blocks),
        {len(ins) - 2: 0, len(ins) - 1: 1},
    )
    output, grad_tokens = call(
        finish_kernel,
        sums,
        [VMEM] * len(sums),
        [piece_shape] * 2,
        [VMEM] * 2,
        [],
        4 * MIB,
        2 * narrow * piece * features,
        4 * narrow * piece * features,
    )
    return (output, grad_tokens, grad_wq, grad_wkv, grad_wo)


def solution(mesh):
    return jax.shard_map(
        functools.partial(shards, mesh.shape["narrow"], mesh.shape["wide"]),
        mesh=mesh,
        in_specs=(
            P("narrow", "wide"),
            P("wide", "narrow"),
            P("wide", "narrow"),
            P("narrow", "wide"),
            P("narrow", "wide"),
        ),
        out_specs=(
            P("narrow", "wide"),
            P("narrow", "wide"),
            P("wide", "narrow"),
            P("wide", "narrow"),
            P("narrow", "wide"),
        ),
        check_vma=False,
    )
```

```python
import functools

import jax
import jax.numpy as jnp
from jax import lax
from jax.experimental import pallas as pl
from jax.experimental.pallas import tpu as pltpu
from jax.sharding import PartitionSpec as P

HD = 128


def contract_rows(left, right):
    return lax.dot_general(
        left, right, (((0,), (0,)), ((), ())), preferred_element_type=jnp.float32
    )


def contract_cols(left, right):
    return lax.dot_general(
        left, right, (((1,), (1,)), ((), ())), preferred_element_type=jnp.float32
    )


def wide_sum(term_fn, all_rows):
    return lax.psum_scatter(
        term_fn(jnp.int32(0), lax.axis_size("wide") * (all_rows // lax.axis_size("wide"))),
        "wide",
        scatter_dimension=0,
        tiled=True,
    )


def row_shards(tokens, w_query, w_keyval, w_output, grad_out):
    wide_index = lax.axis_index("wide")
    token_panel = lax.all_gather(tokens, "narrow", axis=0, tiled=True)
    all_rows = token_panel.shape[0]
    query_cols = w_query.shape[1]
    pair_cols = w_keyval.shape[1]
    joined = jnp.concatenate([w_query, w_keyval], axis=1)

    def project_all(first_row, row_count):
        return jnp.dot(token_panel, joined, preferred_element_type=jnp.float32)

    projected = wide_sum(project_all, all_rows)
    queries = projected[:, :query_cols].astype(jnp.bfloat16)
    kv_own = projected[:, query_cols:].astype(jnp.bfloat16)
    kv_panel = lax.all_gather(kv_own, "wide", axis=0, tiled=True)
    rows_here = queries.shape[0]
    heads_here = query_cols // HD
    groups_here = pair_cols // (2 * HD)
    group_size = heads_here // groups_here
    score_scale = HD ** (-0.5)
    query_pos = wide_index * rows_here + lax.iota(jnp.int32, rows_here)
    key_pos = lax.iota(jnp.int32, all_rows)
    allowed = key_pos[None, :] <= query_pos[:, None]
    query_heads = queries.reshape(rows_here, groups_here, group_size, HD)
    pair_heads = kv_panel.reshape(all_rows, groups_here, 2, HD)
    key_heads = pair_heads[:, :, 0]
    value_heads = pair_heads[:, :, 1]
    scores = (
        jnp.einsum("rghd,sgd->ghrs", query_heads, key_heads, preferred_element_type=jnp.float32)
        * score_scale
    )
    weights = jnp.where(allowed, jnp.exp(scores), 0.0)
    weights = weights / jnp.sum(weights, axis=3, keepdims=True)
    prob_bf = weights.astype(jnp.bfloat16)
    attended = jnp.einsum(
        "ghrs,sgd->rghd", prob_bf, value_heads, preferred_element_type=jnp.float32
    )
    attended = attended.reshape(rows_here, query_cols).astype(jnp.bfloat16)
    att_panel = lax.all_gather(attended, "wide", axis=0, tiled=True)
    row_block = att_panel
    output = lax.psum_scatter(
        jnp.dot(row_block, w_output, preferred_element_type=jnp.float32).astype(jnp.bfloat16),
        "narrow",
        scatter_dimension=0,
        tiled=True,
    )
    grad_panel = lax.all_gather(grad_out, "narrow", axis=0, tiled=True)
    grad_wo = contract_rows(att_panel, grad_panel).astype(jnp.bfloat16)

    def back_out(first_row, row_count):
        return contract_cols(grad_panel, w_output)

    grad_att = wide_sum(back_out, all_rows).astype(jnp.bfloat16)
    grad_heads = grad_att.reshape(rows_here, groups_here, group_size, HD)
    prob_grad = jnp.einsum(
        "rghd,sgd->ghrs", grad_heads, value_heads, preferred_element_type=jnp.float32
    )
    grad_values = jnp.einsum(
        "ghrs,rghd->sgd", prob_bf, grad_heads, preferred_element_type=jnp.float32
    )
    score_grad = weights * (prob_grad - jnp.sum(weights * prob_grad, axis=3, keepdims=True))
    score_half = score_grad.astype(jnp.bfloat16)
    grad_q = (
        jnp.einsum("ghrs,sgd->rghd", score_half, key_heads, preferred_element_type=jnp.float32)
        * score_scale
    )
    grad_q = grad_q.reshape(rows_here, query_cols).astype(jnp.bfloat16)
    grad_keys = (
        jnp.einsum("ghrs,rghd->sgd", score_half, query_heads, preferred_element_type=jnp.float32)
        * score_scale
    )
    kv_grad = jnp.stack([grad_keys, grad_values], axis=2).reshape(all_rows, pair_cols)
    kv_share = lax.psum_scatter(kv_grad, "wide", scatter_dimension=0, tiled=True).astype(
        jnp.bfloat16
    )
    grad_mixed = jnp.concatenate([grad_q, kv_share], axis=1)
    grad_rows = lax.all_gather(grad_mixed, "wide", axis=0, tiled=True)
    grad_joined = contract_rows(token_panel, grad_rows)
    grad_wq = grad_joined[:, :query_cols].astype(jnp.bfloat16)
    grad_wkv = grad_joined[:, query_cols:].astype(jnp.bfloat16)
    row_block = grad_rows
    grad_tokens = lax.psum_scatter(
        contract_cols(row_block, joined).astype(jnp.bfloat16),
        "narrow",
        scatter_dimension=0,
        tiled=True,
    )
    return (output, grad_tokens, grad_wq, grad_wkv, grad_wo)


MIB = 1 << 20
BF = jnp.bfloat16
F32 = jnp.float32
VMEM = pl.BlockSpec(memory_space=pltpu.VMEM)
ANY = pl.BlockSpec(memory_space=pl.ANY)
HBM = pl.BlockSpec(memory_space=pltpu.HBM)


def swap(value, axis, size, distance):
    return lax.ppermute(value, axis, [(i, i ^ distance) for i in range(size)])


def call(kernel, ins, in_specs, outs, out_specs, scratch, vmem, flops, moved, aliases={}):
    return pl.pallas_call(
        kernel,
        out_shape=outs,
        in_specs=in_specs,
        out_specs=out_specs,
        scratch_shapes=scratch,
        input_output_aliases=aliases,
        compiler_params=pltpu.CompilerParams(vmem_limit_bytes=vmem),
        cost_estimate=pl.CostEstimate(flops=flops, bytes_accessed=moved, transcendentals=0),
    )(*ins)


def block_of(distance, cols):
    return pl.ds(pl.multiple_of((lax.axis_index("wide") ^ distance) * cols, cols), cols)


def load_kernel(source, wq, wo, out, sem):
    copy = pltpu.make_async_copy(source, out, sem)
    copy.start()
    copy.wait()


def panels(refs):
    half = len(refs) // 2
    return (jnp.concatenate([r[...] for r in part], axis=0) for part in (refs[:half], refs[half:]))


def query_block(wq, b, cols):
    return wq[:, block_of(b, cols)]


def output_block(wo, b, cols):
    return wo[block_of(b, cols), :]


def project_blocks(token_panel, grad_panel, blocks, wq, wo, width, out):
    cols = width // (2 * len(blocks))
    for at, b in enumerate(blocks):
        left = 2 * at * cols
        out[:, left : left + cols] = jnp.dot(token_panel, query_block(wq, b, cols), preferred_element_type=F32).astype(BF)
        out[:, left + cols : left + 2 * cols] = contract_cols(grad_panel, output_block(wo, b, cols)).astype(BF)


def project_first_kernel(b, count, *refs):
    pieces, (wq, wo, wkv, out, kv) = refs[:count], refs[count:]
    token_panel, grad_panel = panels(pieces)
    kv[...] = jnp.dot(token_panel, wkv[...], preferred_element_type=F32).astype(BF)
    width = out.shape[1] - kv.shape[1]
    out[:, width:] = kv[...]
    project_blocks(token_panel, grad_panel, [b], wq, wo, width, out)


def project_kernel(blocks, count, *refs):
    pieces, (wq, wo, out) = refs[:count], refs[count:]
    token_panel, grad_panel = panels(pieces)
    project_blocks(token_panel, grad_panel, blocks, wq, wo, out.shape[1], out)


def turn_kernel(*refs):
    refs[-1][...] = jnp.concatenate([r[...] for r in refs[:-1]], axis=0).T


def plus(left, right):
    return left.astype(F32) + right.astype(F32)


def total(parts):
    value = parts[0][...].astype(F32)
    for part in parts[1:]:
        value = value + part[...].astype(F32)
    return value


def add_first_kernel(near, kv, far, out, pair):
    width = near.shape[1]
    out[:, :width] = plus(near[...], far[:, :width]).astype(BF)
    pair[...] = plus(kv[...], far[:, width:]).astype(BF)
    out[:, width:] = pair[...]


def add_next_kernel(near, far, pair, out):
    width = near.shape[1]
    out[:, :width] = plus(near[...], far[...]).astype(BF)
    out[:, width:] = pair[...]


def attend_kernel(narrow, near, far, pair, *refs):
    parts, out = refs[:-1], refs[-1]
    value = jnp.concatenate([plus(near[...], far[...]), pair[...].astype(F32)], axis=1)
    value = (value + total(parts)).astype(BF)
    rows = value.shape[0]
    cols = (value.shape[1] - 2 * HD) // 2
    piece = rows // narrow
    me = lax.axis_index("narrow")

    def position(dim):
        at = lax.broadcasted_iota(jnp.int32, (rows, rows), dim)
        return ((at // piece) ^ me) * piece + at % piece

    allowed = position(1) <= position(0)
    keys, values = value[:, 2 * cols : 2 * cols + HD], value[:, 2 * cols + HD :]
    scale = HD ** (-0.5)
    grad_keys = jnp.zeros((rows, HD), F32)
    grad_values = jnp.zeros((rows, HD), F32)
    for at in range(0, cols, HD):
        queries, grads = value[:, at : at + HD], value[:, cols + at : cols + at + HD]
        weights = jnp.where(allowed, jnp.exp(contract_cols(queries, keys) * scale), 0.0)
        weights = weights / jnp.sum(weights, axis=1, keepdims=True)
        probs = weights.astype(BF)
        out[:, at : at + HD] = jnp.dot(probs, values, preferred_element_type=F32).astype(BF)
        prob_grad = contract_cols(grads, values)
        score_grad = weights * (prob_grad - jnp.sum(weights * prob_grad, axis=1, keepdims=True))
        score_half = score_grad.astype(BF)
        out[:, cols + at : cols + at + HD] = (
            jnp.dot(score_half, keys, preferred_element_type=F32) * scale
        ).astype(BF)
        grad_keys = grad_keys + contract_rows(score_half, queries) * scale
        grad_values = grad_values + contract_rows(probs, grads)
    out[:, 2 * cols : 2 * cols + HD] = grad_keys.astype(BF)
    out[:, 2 * cols + HD :] = grad_values.astype(BF)


def join_kernel(width, *refs):
    parts, out = refs[:-1], refs[-1]
    kv = parts[0][:, width:].astype(F32)
    for at, part in enumerate(parts):
        out[:, at * width : (at + 1) * width] = part[:, :width]
        if at:
            kv = kv + part[:, width:].astype(F32)
    out[:, len(parts) * width :] = kv.astype(BF)


def accumulate(blocks, cols, parts, wq, wo, before, out_sum, grad_sum):
    for i, (part, left, b) in enumerate(blocks):
        out = jnp.dot(parts[part][:, left : left + cols], output_block(wo, b, cols), preferred_element_type=F32)
        grad = contract_cols(parts[part][:, left + cols : left + 2 * cols], query_block(wq, b, cols))
        if i == 0 and before:
            out, grad = out + before[0][...], grad + before[1][...]
        elif i:
            out, grad = out + out_sum[...], grad + grad_sum[...]
        out_sum[...] = out
        grad_sum[...] = grad


def back_kernel(blocks, cols, count, *refs):
    parts, (wq, wo), rest = refs[:count], refs[count : count + 2], refs[count + 2 :]
    accumulate(blocks, cols, parts, wq, wo, rest[:-2], *rest[-2:])


def kv_total(parts):
    total = parts[0][:, parts[0].shape[1] - 2 * HD :].astype(F32)
    for part in parts[1:]:
        total = total + part[:, part.shape[1] - 2 * HD :].astype(F32)
    return total.astype(BF)


def back_last_kernel(blocks, cols, count, piece, *refs):
    parts, (wq, wo, wkv, out_before, grad_before, near, far, out_sum, grad_sum) = refs[:count], refs[count:]
    accumulate(blocks, cols, parts, wq, wo, (out_before, grad_before), out_sum, grad_sum)
    grad_sum[...] += contract_cols(kv_total(parts), wkv[...])
    for out, low in ((near, 0), (far, 1)):
        for at in range(out.shape[0] // (2 * piece)):
            first = (2 * at + low) * piece
            out[2 * at * piece : (2 * at + 1) * piece, :] = out_sum[first : first + piece, :].astype(BF)
            out[(2 * at + 1) * piece : (2 * at + 2) * piece, :] = grad_sum[first : first + piece, :].astype(BF)


def send_weight_grads(blocks, cols, turned, grads, parts, gwq, gwo, gwq_v, gwo_v, sems):
    grad_panel = jnp.concatenate([r[...] for r in grads], axis=0)
    copies = []

    def send(source, target):
        copies.append(pltpu.make_async_copy(source, target, sems.at[len(copies)]))
        copies[-1].start()

    tile = 256
    for at, (part, left, b) in enumerate(blocks):
        att = parts[part][:, left : left + cols].T
        for first in range(0, gwo.shape[1], tile):
            span = slice(first, first + tile)
            gwo_v[at, :, span] = jnp.dot(att, grad_panel[:, span], preferred_element_type=F32).astype(BF)
        send(gwo_v.at[at], gwo.at[block_of(b, cols), :])
        grad = parts[part][:, left + cols : left + 2 * cols]
        for first in range(0, gwq.shape[0], tile):
            span = slice(first, first + tile)
            gwq_v[at, span, :] = jnp.dot(turned[span, :], grad, preferred_element_type=F32).astype(BF)
        send(gwq_v.at[at], gwq.at[:, block_of(b, cols)])
    return copies


def block_kernel(blocks, cols, narrow, count, has_before, *refs):
    turned, grads, parts, refs = refs[0], refs[1 : 1 + narrow], refs[1 + narrow : 1 + narrow + count], refs[1 + narrow + count :]
    wq, wo = refs[:2]
    before, outs = (refs[2:4], refs[6:]) if has_before else ((), refs[2:])
    gwq, gwo, out_sum, grad_sum, gwq_v, gwo_v, sems = outs
    copies = send_weight_grads(blocks, cols, turned, grads, parts, gwq, gwo, gwq_v, gwo_v, sems)
    accumulate(blocks, cols, parts, wq, wo, before, out_sum, grad_sum)
    for copy in copies:
        copy.wait()


def weight_grad_kernel(blocks, cols, narrow, count, *refs):
    turned, grads, parts = refs[0], refs[1 : 1 + narrow], refs[1 + narrow : 1 + narrow + count]
    gwq, gwo, gwkv, gwkv_v, gwq_v, gwo_v, sems = refs[3 + narrow + count :]
    gwkv_v[...] = jnp.dot(turned[...], kv_total(parts), preferred_element_type=F32).astype(BF)
    last = pltpu.make_async_copy(gwkv_v, gwkv, sems.at[2 * len(blocks)])
    last.start()
    copies = send_weight_grads(blocks, cols, turned, grads, parts, gwq, gwo, gwq_v, gwo_v, sems)
    for copy in copies + [last]:
        copy.wait()


def add_pieces_kernel(near, far, own, *outs):
    rows = own.shape[0]
    for at, out in enumerate((own,) + outs):
        part = slice(at * rows, (at + 1) * rows)
        out[...] = plus(near[part, :], far[part, :]).astype(BF)


def finish_kernel(*refs):
    parts, output, grad = refs[:-2], refs[-2], refs[-1]
    value = total(parts)
    rows = output.shape[0]
    output[...] = value[:rows].astype(BF)
    grad[...] = value[rows:].astype(BF)


def shards(narrow, wide, tokens, w_query, w_keyval, w_output, grad_out):
    piece, features = tokens.shape
    query_cols, pair_cols = w_query.shape[1], w_keyval.shape[1]
    cols = query_cols // wide
    if pair_cols != 2 * HD or cols % HD or cols * wide != query_cols or piece % 16 or narrow & (narrow - 1) or wide & (wide - 1) or wide < 8 or narrow < 2:
        return row_shards(tokens, w_query, w_keyval, w_output, grad_out)
    rows = narrow * piece
    weight_size = features * (2 * query_cols + pair_cols)
    full = jax.ShapeDtypeStruct((rows, 2 * cols + pair_cols), BF)
    piece_shape = jax.ShapeDtypeStruct((piece, features), BF)
    half = wide // 2
    sems = pltpu.SemaphoreType.DMA((4 * wide,))

    def spread(value):
        pieces = {0: value}
        bit = narrow // 2
        while bit > 1:
            pieces.update({b ^ bit: swap(p, "narrow", narrow, bit) for b, p in pieces.items()})
            bit //= 2
        return {b: p for b, p in pieces.items() if b}

    token_pieces, grad_pieces = spread(tokens), spread(grad_out)
    beside = [{0: v, 1: swap(v, "narrow", narrow, 1)} for v in (tokens, grad_out)]
    far_blocks = list(range(wide - 1, 0, -2))
    near_blocks = list(range(wide - 2, -1, -2))
    wkv = call(
        load_kernel,
        [pltpu.with_memory_space_constraint(w, pltpu.HBM) for w in (w_keyval, w_query, w_output)],
        [HBM] * 3,
        jax.ShapeDtypeStruct(w_keyval.shape, BF),
        VMEM,
        [pltpu.SemaphoreType.DMA],
        2 * MIB,
        0,
        2 * weight_size,
    )
    token_pieces, grad_pieces, wkv = lax.optimization_barrier((token_pieces, grad_pieces, wkv))
    for pieces in (token_pieces, grad_pieces):
        pieces.update({b ^ 1: swap(p, "narrow", narrow, 1) for b, p in pieces.items() if b})
    token_pieces, grad_pieces = [[{**own, **p}[b] for b in range(narrow)] for own, p in zip(beside, (token_pieces, grad_pieces))]
    most = half - 1
    pieces = (*token_pieces, *grad_pieces)
    count = 2 * narrow

    def project(block, pieces=pieces):
        return call(
            functools.partial(project_kernel, [block], count),
            (*pieces, w_query, w_output),
            [VMEM] * (count + 2),
            jax.ShapeDtypeStruct((rows, 2 * cols), BF),
            VMEM,
            [],
            8 * MIB,
            4 * rows * features * cols,
            4 * features * cols,
        )

    far, kv = call(
        functools.partial(project_first_kernel, far_blocks[0], count),
        (*pieces, w_query, w_output, wkv),
        [VMEM] * (count + 3),
        [full, jax.ShapeDtypeStruct((rows, pair_cols), BF)],
        [VMEM] * 2,
        [],
        8 * MIB,
        2 * rows * features * (2 * cols + pair_cols),
        2 * features * (2 * cols + pair_cols),
    )
    far = [swap(far, "wide", wide, 1)] + [swap(project(b), "wide", wide, 1) for b in far_blocks[1:most]]
    sums, pair = [], None
    for at in range(most):
        near = project(near_blocks[at])
        added, *rest = call(
            add_next_kernel if sums else add_first_kernel,
            (near, far[at], pair) if sums else (near, kv, far[at]),
            [VMEM] * 3,
            [full] if sums else [full, jax.ShapeDtypeStruct((rows, pair_cols), BF)],
            [VMEM] * (1 if sums else 2),
            [],
            2 * MIB,
            rows * 1024,
            rows * 4096,
        )
        pair = rest[0] if rest else pair
        sums.append(added)
    received = [swap(part, "wide", wide, d) for part, d in zip(sums, near_blocks)]
    far_last = swap(project(far_blocks[most]), "wide", wide, 1)
    later, _ = lax.optimization_barrier((pieces, sums[-1]))
    near_last = project(near_blocks[most], later)
    turned = call(
        turn_kernel,
        later[:narrow],
        [VMEM] * narrow,
        jax.ShapeDtypeStruct((features, rows), BF),
        VMEM,
        [],
        2 * MIB,
        0,
        4 * rows * features,
    )
    near_last, turned = lax.optimization_barrier((near_last, turned))
    own = call(
        functools.partial(attend_kernel, narrow),
        (near_last, far_last, pair, *received),
        [VMEM] * (3 + len(received)),
        full,
        VMEM,
        [],
        4 * MIB,
        24 * rows * rows * cols,
        2 * rows * wide * full.shape[1],
    )
    width = 2 * cols
    same = {0: own, **{d: swap(own, "wide", wide, d) for d in near_blocks[:-1]}}
    width = 2 * cols
    sum_shapes = [jax.ShapeDtypeStruct((rows, features), F32)] * 2
    grad_shapes = [jax.ShapeDtypeStruct(w.shape, BF) for w in (w_query, w_output)]

    def grad_scratch(blocks):
        return [pltpu.VMEM((len(blocks), features, cols), BF), pltpu.VMEM((len(blocks), cols, features), BF), sems]

    def block_terms(distances, before=()):
        blocks = [(i, 0, d) for i, d in enumerate(distances)]
        ins = (turned, *grad_pieces, *[same[d] for d in distances], w_query, w_output, *before)
        return call(
            functools.partial(block_kernel, blocks, cols, narrow, len(blocks), bool(before)),
            ins,
            [VMEM] * (3 + narrow + len(blocks)) + ([VMEM] * 2 + [ANY] * 2 if before else []),
            grad_shapes + sum_shapes,
            [ANY] * 2 + [VMEM] * 2,
            grad_scratch(blocks),
            20 * MIB,
            8 * rows * features * cols * len(blocks),
            8 * features * cols * len(blocks),
            {len(ins) - 2: 0, len(ins) - 1: 1} if before else {},
        )

    same = {0: own, **{d: swap(own, "wide", wide, d) for d in near_blocks[:-1]}}
    first, rest = near_blocks[-2], near_blocks[:-2]
    groups = ([0, first], rest)
    joined = []
    for group in groups:
        if joined:
            *grads, out_sum, grad_sum = block_terms([0, first])
            same[rest[-1]], grads, out_sum, grad_sum = lax.optimization_barrier((same[rest[-1]], grads, out_sum, grad_sum))
        together = call(
            functools.partial(join_kernel, width),
            [same[d] for d in group],
            [VMEM] * len(group),
            jax.ShapeDtypeStruct((rows, width * len(group) + pair_cols), BF),
            VMEM,
            [],
            2 * MIB,
            0,
            4 * rows * full.shape[1] * len(group),
        )
        joined.append(swap(together, "wide", wide, 1))
    *grads, out_sum, grad_sum = block_terms(rest, (out_sum, grad_sum, *grads))
    blocks = [[(i, width * at, d + 1) for at, d in enumerate(group)] for i, group in enumerate(groups)]
    out_sum, grad_sum = call(
        functools.partial(back_kernel, blocks[0], cols, 1),
        (joined[0], w_query, w_output, out_sum, grad_sum),
        [VMEM] * 5,
        sum_shapes,
        [VMEM] * 2,
        [],
        8 * MIB,
        4 * rows * features * cols * len(blocks[0]),
        4 * features * cols * len(blocks[0]),
    )
    parts = [*joined, *same.values()]
    piece_half = jax.ShapeDtypeStruct((narrow * piece, features), BF)
    piece_pair = jax.ShapeDtypeStruct((2 * piece, features), BF)
    near, far = call(
        functools.partial(back_last_kernel, blocks[1], cols, len(parts), piece),
        (*parts, w_query, w_output, wkv, out_sum, grad_sum),
        [VMEM] * (len(parts) + 5),
        [piece_half] * 2,
        [VMEM] * 2,
        [pltpu.VMEM((rows, features), F32), pltpu.VMEM((rows, features), F32)],
        8 * MIB,
        rows * weight_size,
        weight_size,
    )
    far = swap(far, "narrow", narrow, 1)
    sums = call(
        add_pieces_kernel,
        (near, far),
        [VMEM] * 2,
        [piece_pair] * (narrow // 2),
        [VMEM] * (narrow // 2),
        [],
        2 * MIB,
        2 * rows * features,
        12 * rows * features,
    )
    sums = [sums[0]] + [swap(sums[i], "narrow", narrow, 2 * i) for i in range(1, narrow // 2)]
    blocks = blocks[0] + blocks[1]
    ins = (turned, *grad_pieces, *parts, *grads)
    grad_wq, grad_wo, grad_wkv = call(
        functools.partial(weight_grad_kernel, blocks, cols, narrow, len(parts)),
        ins,
        [VMEM] * (1 + narrow + len(parts)) + [ANY] * 2,
        grad_shapes + [jax.ShapeDtypeStruct(w_keyval.shape, BF)],
        [ANY] * 3,
        [pltpu.VMEM(w_keyval.shape, BF)] + grad_scratch(blocks),
        20 * MIB,
        8 * rows * features * cols * len(blocks),
        8 * features * cols * len(blocks),
        {len(ins) - 2: 0, len(ins) - 1: 1},
    )
    output, grad_tokens = call(
        finish_kernel,
        sums,
        [VMEM] * len(sums),
        [piece_shape] * 2,
        [VMEM] * 2,
        [],
        4 * MIB,
        2 * narrow * piece * features,
        4 * narrow * piece * features,
    )
    return (output, grad_tokens, grad_wq, grad_wkv, grad_wo)


def solution(mesh):
    return jax.shard_map(
        functools.partial(shards, mesh.shape["narrow"], mesh.shape["wide"]),
        mesh=mesh,
        in_specs=(
            P("narrow", "wide"),
            P("wide", "narrow"),
            P("wide", "narrow"),
            P("narrow", "wide"),
            P("narrow", "wide"),
        ),
        out_specs=(
            P("narrow", "wide"),
            P("narrow", "wide"),
            P("wide", "narrow"),
            P("wide", "narrow"),
            P("narrow", "wide"),
        ),
        check_vma=False,
    )
```

```python
import functools

import jax
import jax.numpy as jnp
from jax import lax
from jax.experimental import pallas as pl
from jax.experimental.pallas import tpu as pltpu
from jax.sharding import PartitionSpec as P

HD = 128


def contract_rows(left, right):
    return lax.dot_general(
        left, right, (((0,), (0,)), ((), ())), preferred_element_type=jnp.float32
    )


def contract_cols(left, right):
    return lax.dot_general(
        left, right, (((1,), (1,)), ((), ())), preferred_element_type=jnp.float32
    )


def wide_sum(term_fn, all_rows):
    return lax.psum_scatter(
        term_fn(jnp.int32(0), lax.axis_size("wide") * (all_rows // lax.axis_size("wide"))),
        "wide",
        scatter_dimension=0,
        tiled=True,
    )


def row_shards(tokens, w_query, w_keyval, w_output, grad_out):
    wide_index = lax.axis_index("wide")
    token_panel = lax.all_gather(tokens, "narrow", axis=0, tiled=True)
    all_rows = token_panel.shape[0]
    query_cols = w_query.shape[1]
    pair_cols = w_keyval.shape[1]
    joined = jnp.concatenate([w_query, w_keyval], axis=1)

    def project_all(first_row, row_count):
        return jnp.dot(token_panel, joined, preferred_element_type=jnp.float32)

    projected = wide_sum(project_all, all_rows)
    queries = projected[:, :query_cols].astype(jnp.bfloat16)
    kv_own = projected[:, query_cols:].astype(jnp.bfloat16)
    kv_panel = lax.all_gather(kv_own, "wide", axis=0, tiled=True)
    rows_here = queries.shape[0]
    heads_here = query_cols // HD
    groups_here = pair_cols // (2 * HD)
    group_size = heads_here // groups_here
    score_scale = HD ** (-0.5)
    query_pos = wide_index * rows_here + lax.iota(jnp.int32, rows_here)
    key_pos = lax.iota(jnp.int32, all_rows)
    allowed = key_pos[None, :] <= query_pos[:, None]
    query_heads = queries.reshape(rows_here, groups_here, group_size, HD)
    pair_heads = kv_panel.reshape(all_rows, groups_here, 2, HD)
    key_heads = pair_heads[:, :, 0]
    value_heads = pair_heads[:, :, 1]
    scores = (
        jnp.einsum("rghd,sgd->ghrs", query_heads, key_heads, preferred_element_type=jnp.float32)
        * score_scale
    )
    weights = jnp.where(allowed, jnp.exp(scores), 0.0)
    weights = weights / jnp.sum(weights, axis=3, keepdims=True)
    prob_bf = weights.astype(jnp.bfloat16)
    attended = jnp.einsum(
        "ghrs,sgd->rghd", prob_bf, value_heads, preferred_element_type=jnp.float32
    )
    attended = attended.reshape(rows_here, query_cols).astype(jnp.bfloat16)
    att_panel = lax.all_gather(attended, "wide", axis=0, tiled=True)
    row_block = att_panel
    output = lax.psum_scatter(
        jnp.dot(row_block, w_output, preferred_element_type=jnp.float32).astype(jnp.bfloat16),
        "narrow",
        scatter_dimension=0,
        tiled=True,
    )
    grad_panel = lax.all_gather(grad_out, "narrow", axis=0, tiled=True)
    grad_wo = contract_rows(att_panel, grad_panel).astype(jnp.bfloat16)

    def back_out(first_row, row_count):
        return contract_cols(grad_panel, w_output)

    grad_att = wide_sum(back_out, all_rows).astype(jnp.bfloat16)
    grad_heads = grad_att.reshape(rows_here, groups_here, group_size, HD)
    prob_grad = jnp.einsum(
        "rghd,sgd->ghrs", grad_heads, value_heads, preferred_element_type=jnp.float32
    )
    grad_values = jnp.einsum(
        "ghrs,rghd->sgd", prob_bf, grad_heads, preferred_element_type=jnp.float32
    )
    score_grad = weights * (prob_grad - jnp.sum(weights * prob_grad, axis=3, keepdims=True))
    score_half = score_grad.astype(jnp.bfloat16)
    grad_q = (
        jnp.einsum("ghrs,sgd->rghd", score_half, key_heads, preferred_element_type=jnp.float32)
        * score_scale
    )
    grad_q = grad_q.reshape(rows_here, query_cols).astype(jnp.bfloat16)
    grad_keys = (
        jnp.einsum("ghrs,rghd->sgd", score_half, query_heads, preferred_element_type=jnp.float32)
        * score_scale
    )
    kv_grad = jnp.stack([grad_keys, grad_values], axis=2).reshape(all_rows, pair_cols)
    kv_share = lax.psum_scatter(kv_grad, "wide", scatter_dimension=0, tiled=True).astype(
        jnp.bfloat16
    )
    grad_mixed = jnp.concatenate([grad_q, kv_share], axis=1)
    grad_rows = lax.all_gather(grad_mixed, "wide", axis=0, tiled=True)
    grad_joined = contract_rows(token_panel, grad_rows)
    grad_wq = grad_joined[:, :query_cols].astype(jnp.bfloat16)
    grad_wkv = grad_joined[:, query_cols:].astype(jnp.bfloat16)
    row_block = grad_rows
    grad_tokens = lax.psum_scatter(
        contract_cols(row_block, joined).astype(jnp.bfloat16),
        "narrow",
        scatter_dimension=0,
        tiled=True,
    )
    return (output, grad_tokens, grad_wq, grad_wkv, grad_wo)


MIB = 1 << 20
BF = jnp.bfloat16
F32 = jnp.float32
VMEM = pl.BlockSpec(memory_space=pltpu.VMEM)
ANY = pl.BlockSpec(memory_space=pl.ANY)
HBM = pl.BlockSpec(memory_space=pltpu.HBM)


def swap(value, axis, size, distance):
    return lax.ppermute(value, axis, [(i, i ^ distance) for i in range(size)])


def call(kernel, ins, in_specs, outs, out_specs, scratch, vmem, flops, moved, aliases={}):
    return pl.pallas_call(
        kernel,
        out_shape=outs,
        in_specs=in_specs,
        out_specs=out_specs,
        scratch_shapes=scratch,
        input_output_aliases=aliases,
        compiler_params=pltpu.CompilerParams(vmem_limit_bytes=vmem),
        cost_estimate=pl.CostEstimate(flops=flops, bytes_accessed=moved, transcendentals=0),
    )(*ins)


def block_of(distance, cols):
    return pl.ds(pl.multiple_of((lax.axis_index("wide") ^ distance) * cols, cols), cols)


def load_kernel(source, wq, wo, out, sem):
    copy = pltpu.make_async_copy(source, out, sem)
    copy.start()
    copy.wait()


def panels(refs):
    half = len(refs) // 2
    return (jnp.concatenate([r[...] for r in part], axis=0) for part in (refs[:half], refs[half:]))


def query_block(wq, b, cols):
    return wq[:, block_of(b, cols)]


def output_block(wo, b, cols):
    return wo[block_of(b, cols), :]


def project_blocks(token_panel, grad_panel, blocks, wq, wo, width, out):
    cols = width // (2 * len(blocks))
    for at, b in enumerate(blocks):
        left = 2 * at * cols
        out[:, left : left + cols] = jnp.dot(token_panel, query_block(wq, b, cols), preferred_element_type=F32).astype(BF)
        out[:, left + cols : left + 2 * cols] = contract_cols(grad_panel, output_block(wo, b, cols)).astype(BF)


def query_columns(panel, blocks, wq, out):
    cols = out.shape[1] // len(blocks)
    for at, b in enumerate(blocks):
        out[:, at * cols : (at + 1) * cols] = jnp.dot(panel, query_block(wq, b, cols), preferred_element_type=F32).astype(BF)


def project_first_kernel(blocks, count, *refs):
    pieces, (wq, wkv, out, kv) = refs[:count], refs[count:]
    panel = jnp.concatenate([r[...] for r in pieces], axis=0)
    kv[...] = jnp.dot(panel, wkv[...], preferred_element_type=F32).astype(BF)
    query_columns(panel, blocks, wq, out)


def project_query_kernel(blocks, count, *refs):
    pieces, (wq, out) = refs[:count], refs[count:]
    query_columns(jnp.concatenate([r[...] for r in pieces], axis=0), blocks, wq, out)


def join_block_kernel(b, at, count, *refs):
    pieces, (wo, queries, *kv, out) = refs[:count], refs[count:]
    cols = wo.shape[0] // lax.axis_size("wide")
    out[:, :cols] = queries[:, at * cols : (at + 1) * cols]
    panel = jnp.concatenate([r[...] for r in pieces], axis=0)
    out[:, cols : 2 * cols] = contract_cols(panel, output_block(wo, b, cols)).astype(BF)
    if kv:
        out[:, 2 * cols :] = kv[0][...]


def project_kernel(blocks, count, *refs):
    pieces, (wq, wo, out) = refs[:count], refs[count:]
    token_panel, grad_panel = panels(pieces)
    project_blocks(token_panel, grad_panel, blocks, wq, wo, out.shape[1], out)


def turn_kernel(*refs):
    refs[-1][...] = jnp.concatenate([r[...] for r in refs[:-1]], axis=0).T


def plus(left, right):
    return left.astype(F32) + right.astype(F32)


def total(parts):
    value = parts[0][...].astype(F32)
    for part in parts[1:]:
        value = value + part[...].astype(F32)
    return value


def add_first_kernel(near, kv, far, out, pair):
    width = near.shape[1]
    out[:, :width] = plus(near[...], far[:, :width]).astype(BF)
    pair[...] = plus(kv[...], far[:, width:]).astype(BF)
    out[:, width:] = pair[...]


def add_next_kernel(near, far, pair, out):
    width = near.shape[1]
    out[:, :width] = plus(near[...], far[...]).astype(BF)
    out[:, width:] = pair[...]


def attend_kernel(narrow, near, far, pair, *refs):
    parts, out = refs[:-1], refs[-1]
    value = jnp.concatenate([plus(near[...], far[...]), pair[...].astype(F32)], axis=1)
    value = (value + total(parts)).astype(BF)
    rows = value.shape[0]
    cols = (value.shape[1] - 2 * HD) // 2
    piece = rows // narrow
    me = lax.axis_index("narrow")

    def position(dim):
        at = lax.broadcasted_iota(jnp.int32, (rows, rows), dim)
        return ((at // piece) ^ me) * piece + at % piece

    allowed = position(1) <= position(0)
    keys, values = value[:, 2 * cols : 2 * cols + HD], value[:, 2 * cols + HD :]
    scale = HD ** (-0.5)
    grad_keys = jnp.zeros((rows, HD), F32)
    grad_values = jnp.zeros((rows, HD), F32)
    for at in range(0, cols, HD):
        queries, grads = value[:, at : at + HD], value[:, cols + at : cols + at + HD]
        weights = jnp.where(allowed, jnp.exp(contract_cols(queries, keys) * scale), 0.0)
        weights = weights / jnp.sum(weights, axis=1, keepdims=True)
        probs = weights.astype(BF)
        out[:, at : at + HD] = jnp.dot(probs, values, preferred_element_type=F32).astype(BF)
        prob_grad = contract_cols(grads, values)
        score_grad = weights * (prob_grad - jnp.sum(weights * prob_grad, axis=1, keepdims=True))
        score_half = score_grad.astype(BF)
        out[:, cols + at : cols + at + HD] = (
            jnp.dot(score_half, keys, preferred_element_type=F32) * scale
        ).astype(BF)
        grad_keys = grad_keys + contract_rows(score_half, queries) * scale
        grad_values = grad_values + contract_rows(probs, grads)
    out[:, 2 * cols : 2 * cols + HD] = grad_keys.astype(BF)
    out[:, 2 * cols + HD :] = grad_values.astype(BF)


def join_kernel(width, *refs):
    parts, out = refs[:-1], refs[-1]
    kv = parts[0][:, width:].astype(F32)
    for at, part in enumerate(parts):
        out[:, at * width : (at + 1) * width] = part[:, :width]
        if at:
            kv = kv + part[:, width:].astype(F32)
    out[:, len(parts) * width :] = kv.astype(BF)


def accumulate(blocks, cols, parts, wq, wo, before, out_sum, grad_sum):
    for i, (part, left, b) in enumerate(blocks):
        out = jnp.dot(parts[part][:, left : left + cols], output_block(wo, b, cols), preferred_element_type=F32)
        grad = contract_cols(parts[part][:, left + cols : left + 2 * cols], query_block(wq, b, cols))
        if i == 0 and before:
            out, grad = out + before[0][...], grad + before[1][...]
        elif i:
            out, grad = out + out_sum[...], grad + grad_sum[...]
        out_sum[...] = out
        grad_sum[...] = grad


def back_kernel(blocks, cols, count, *refs):
    parts, (wq, wo), rest = refs[:count], refs[count : count + 2], refs[count + 2 :]
    accumulate(blocks, cols, parts, wq, wo, rest[:-2], *rest[-2:])


def kv_total(parts):
    total = parts[0][:, parts[0].shape[1] - 2 * HD :].astype(F32)
    for part in parts[1:]:
        total = total + part[:, part.shape[1] - 2 * HD :].astype(F32)
    return total.astype(BF)


def back_last_kernel(blocks, cols, count, piece, *refs):
    parts, (wq, wo, wkv, out_before, grad_before, near, far, out_sum, grad_sum) = refs[:count], refs[count:]
    accumulate(blocks, cols, parts, wq, wo, (out_before, grad_before), out_sum, grad_sum)
    grad_sum[...] += contract_cols(kv_total(parts), wkv[...])
    for out, low in ((near, 0), (far, 1)):
        for at in range(out.shape[0] // (2 * piece)):
            first = (2 * at + low) * piece
            out[2 * at * piece : (2 * at + 1) * piece, :] = out_sum[first : first + piece, :].astype(BF)
            out[(2 * at + 1) * piece : (2 * at + 2) * piece, :] = grad_sum[first : first + piece, :].astype(BF)


def send_weight_grads(blocks, cols, turned, grads, parts, gwq, gwo, gwq_v, gwo_v, sems):
    grad_panel = jnp.concatenate([r[...] for r in grads], axis=0)
    copies = []

    def send(source, target):
        copies.append(pltpu.make_async_copy(source, target, sems.at[len(copies)]))
        copies[-1].start()

    tile = 256
    for at, (part, left, b) in enumerate(blocks):
        att = parts[part][:, left : left + cols].T
        for first in range(0, gwo.shape[1], tile):
            span = slice(first, first + tile)
            gwo_v[at, :, span] = jnp.dot(att, grad_panel[:, span], preferred_element_type=F32).astype(BF)
        send(gwo_v.at[at], gwo.at[block_of(b, cols), :])
        grad = parts[part][:, left + cols : left + 2 * cols]
        for first in range(0, gwq.shape[0], tile):
            span = slice(first, first + tile)
            gwq_v[at, span, :] = jnp.dot(turned[span, :], grad, preferred_element_type=F32).astype(BF)
        send(gwq_v.at[at], gwq.at[:, block_of(b, cols)])
    return copies


def block_kernel(blocks, cols, narrow, count, has_before, *refs):
    turned, grads, parts, refs = refs[0], refs[1 : 1 + narrow], refs[1 + narrow : 1 + narrow + count], refs[1 + narrow + count :]
    wq, wo = refs[:2]
    before, outs = (refs[2:4], refs[6:]) if has_before else ((), refs[2:])
    gwq, gwo, out_sum, grad_sum, gwq_v, gwo_v, sems = outs
    copies = send_weight_grads(blocks, cols, turned, grads, parts, gwq, gwo, gwq_v, gwo_v, sems)
    accumulate(blocks, cols, parts, wq, wo, before, out_sum, grad_sum)
    for copy in copies:
        copy.wait()


def weight_grad_kernel(blocks, cols, narrow, count, *refs):
    turned, grads, parts = refs[0], refs[1 : 1 + narrow], refs[1 + narrow : 1 + narrow + count]
    gwq, gwo, gwkv, gwkv_v, gwq_v, gwo_v, sems = refs[3 + narrow + count :]
    gwkv_v[...] = jnp.dot(turned[...], kv_total(parts), preferred_element_type=F32).astype(BF)
    last = pltpu.make_async_copy(gwkv_v, gwkv, sems.at[2 * len(blocks)])
    last.start()
    copies = send_weight_grads(blocks, cols, turned, grads, parts, gwq, gwo, gwq_v, gwo_v, sems)
    for copy in copies + [last]:
        copy.wait()


def add_pieces_kernel(near, far, own, *outs):
    rows = own.shape[0]
    for at, out in enumerate((own,) + outs):
        part = slice(at * rows, (at + 1) * rows)
        out[...] = plus(near[part, :], far[part, :]).astype(BF)


def finish_kernel(*refs):
    parts, output, grad = refs[:-2], refs[-2], refs[-1]
    value = total(parts)
    rows = output.shape[0]
    output[...] = value[:rows].astype(BF)
    grad[...] = value[rows:].astype(BF)


def shards(narrow, wide, tokens, w_query, w_keyval, w_output, grad_out):
    piece, features = tokens.shape
    query_cols, pair_cols = w_query.shape[1], w_keyval.shape[1]
    cols = query_cols // wide
    if pair_cols != 2 * HD or cols % HD or cols * wide != query_cols or piece % 16 or narrow & (narrow - 1) or wide & (wide - 1) or wide < 8 or narrow < 2:
        return row_shards(tokens, w_query, w_keyval, w_output, grad_out)
    rows = narrow * piece
    weight_size = features * (2 * query_cols + pair_cols)
    full = jax.ShapeDtypeStruct((rows, 2 * cols + pair_cols), BF)
    piece_shape = jax.ShapeDtypeStruct((piece, features), BF)
    half = wide // 2
    sems = pltpu.SemaphoreType.DMA((4 * wide,))

    def spread(value):
        pieces = {0: value}
        bit = narrow // 2
        while bit > 1:
            pieces.update({b ^ bit: swap(p, "narrow", narrow, bit) for b, p in pieces.items()})
            bit //= 2
        return {b: p for b, p in pieces.items() if b}

    token_pieces, grad_pieces = spread(tokens), spread(grad_out)
    beside = [{0: v, 1: swap(v, "narrow", narrow, 1)} for v in (tokens, grad_out)]
    far_blocks = list(range(wide - 1, 0, -2))
    near_blocks = list(range(wide - 2, -1, -2))
    wkv = call(
        load_kernel,
        [pltpu.with_memory_space_constraint(w, pltpu.HBM) for w in (w_keyval, w_query, w_output)],
        [HBM] * 3,
        jax.ShapeDtypeStruct(w_keyval.shape, BF),
        VMEM,
        [pltpu.SemaphoreType.DMA],
        2 * MIB,
        0,
        2 * weight_size,
    )
    def complete(pieces, own, behind):
        pieces, _ = lax.optimization_barrier((pieces, behind))
        pieces = {**own, **pieces}
        pieces.update({b ^ 1: swap(p, "narrow", narrow, 1) for b, p in pieces.items() if b > 1})
        return [pieces[b] for b in range(narrow)]

    token_pieces = complete(token_pieces, beside[0], wkv)
    kv_shape = jax.ShapeDtypeStruct((rows, pair_cols), BF)
    query_first, kv = call(
        functools.partial(project_first_kernel, far_blocks[:1], narrow),
        (*token_pieces, w_query, wkv),
        [VMEM] * (narrow + 2),
        [jax.ShapeDtypeStruct((rows, cols), BF), kv_shape],
        [VMEM] * 2,
        [],
        8 * MIB,
        2 * rows * features * (cols + pair_cols),
        2 * features * (cols + pair_cols),
    )
    grad_pieces = complete(grad_pieces, beside[1], wkv)
    query_rest = call(
        functools.partial(project_query_kernel, far_blocks[1:], narrow),
        (*token_pieces, w_query),
        [VMEM] * (narrow + 1),
        jax.ShapeDtypeStruct((rows, cols * (half - 1)), BF),
        VMEM,
        [],
        8 * MIB,
        2 * rows * features * cols * (half - 1),
        2 * features * cols * (half - 1),
    )
    most = half - 1
    pieces = (*token_pieces, *grad_pieces)
    count = 2 * narrow

    def project(block, pieces=pieces):
        return call(
            functools.partial(project_kernel, [block], count),
            (*pieces, w_query, w_output),
            [VMEM] * (count + 2),
            jax.ShapeDtypeStruct((rows, 2 * cols), BF),
            VMEM,
            [],
            8 * MIB,
            4 * rows * features * cols,
            4 * features * cols,
        )

    def far_swap(at):
        queries = (query_rest,) if at else (query_first, kv)
        block = call(
            functools.partial(join_block_kernel, far_blocks[at], max(at - 1, 0), narrow),
            (*grad_pieces, w_output, *queries),
            [VMEM] * (narrow + 1 + len(queries)),
            jax.ShapeDtypeStruct((rows, 2 * cols + (0 if at else pair_cols)), BF),
            VMEM,
            [],
            8 * MIB,
            2 * rows * features * cols,
            2 * features * cols,
        )
        return swap(block, "wide", wide, 1)

    far = [far_swap(at) for at in range(most)]
    sums, pair = [], None
    for at in range(most):
        near = project(near_blocks[at])
        added, *rest = call(
            add_next_kernel if sums else add_first_kernel,
            (near, far[at], pair) if sums else (near, kv, far[at]),
            [VMEM] * 3,
            [full] if sums else [full, jax.ShapeDtypeStruct((rows, pair_cols), BF)],
            [VMEM] * (1 if sums else 2),
            [],
            2 * MIB,
            rows * 1024,
            rows * 4096,
        )
        pair = rest[0] if rest else pair
        sums.append(added)
    received = [swap(part, "wide", wide, d) for part, d in zip(sums, near_blocks)]
    far_last = far_swap(most)
    later, _ = lax.optimization_barrier((pieces, sums[-1]))
    near_last = project(near_blocks[most], later)
    turned = call(
        turn_kernel,
        later[:narrow],
        [VMEM] * narrow,
        jax.ShapeDtypeStruct((features, rows), BF),
        VMEM,
        [],
        2 * MIB,
        0,
        4 * rows * features,
    )
    near_last, turned = lax.optimization_barrier((near_last, turned))
    own = call(
        functools.partial(attend_kernel, narrow),
        (near_last, far_last, pair, *received),
        [VMEM] * (3 + len(received)),
        full,
        VMEM,
        [],
        4 * MIB,
        24 * rows * rows * cols,
        2 * rows * wide * full.shape[1],
    )
    width = 2 * cols
    same = {0: own, **{d: swap(own, "wide", wide, d) for d in near_blocks[:-1]}}
    width = 2 * cols
    sum_shapes = [jax.ShapeDtypeStruct((rows, features), F32)] * 2
    grad_shapes = [jax.ShapeDtypeStruct(w.shape, BF) for w in (w_query, w_output)]

    def grad_scratch(blocks):
        return [pltpu.VMEM((len(blocks), features, cols), BF), pltpu.VMEM((len(blocks), cols, features), BF), sems]

    def block_terms(distances, before=()):
        blocks = [(i, 0, d) for i, d in enumerate(distances)]
        ins = (turned, *grad_pieces, *[same[d] for d in distances], w_query, w_output, *before)
        return call(
            functools.partial(block_kernel, blocks, cols, narrow, len(blocks), bool(before)),
            ins,
            [VMEM] * (3 + narrow + len(blocks)) + ([VMEM] * 2 + [ANY] * 2 if before else []),
            grad_shapes + sum_shapes,
            [ANY] * 2 + [VMEM] * 2,
            grad_scratch(blocks),
            20 * MIB,
            8 * rows * features * cols * len(blocks),
            8 * features * cols * len(blocks),
            {len(ins) - 2: 0, len(ins) - 1: 1} if before else {},
        )

    same = {0: own, **{d: swap(own, "wide", wide, d) for d in near_blocks[:-1]}}
    first, rest = near_blocks[-2], near_blocks[:-2]
    groups = ([0, first], rest)
    joined = []
    for group in groups:
        if joined:
            *grads, out_sum, grad_sum = block_terms([0, first])
            same[rest[-1]], grads, out_sum, grad_sum = lax.optimization_barrier((same[rest[-1]], grads, out_sum, grad_sum))
        together = call(
            functools.partial(join_kernel, width),
            [same[d] for d in group],
            [VMEM] * len(group),
            jax.ShapeDtypeStruct((rows, width * len(group) + pair_cols), BF),
            VMEM,
            [],
            2 * MIB,
            0,
            4 * rows * full.shape[1] * len(group),
        )
        joined.append(swap(together, "wide", wide, 1))
    *grads, out_sum, grad_sum = block_terms(rest, (out_sum, grad_sum, *grads))
    blocks = [[(i, width * at, d + 1) for at, d in enumerate(group)] for i, group in enumerate(groups)]
    out_sum, grad_sum = call(
        functools.partial(back_kernel, blocks[0], cols, 1),
        (joined[0], w_query, w_output, out_sum, grad_sum),
        [VMEM] * 5,
        sum_shapes,
        [VMEM] * 2,
        [],
        8 * MIB,
        4 * rows * features * cols * len(blocks[0]),
        4 * features * cols * len(blocks[0]),
    )
    parts = [*joined, *same.values()]
    piece_half = jax.ShapeDtypeStruct((narrow * piece, features), BF)
    piece_pair = jax.ShapeDtypeStruct((2 * piece, features), BF)
    near, far = call(
        functools.partial(back_last_kernel, blocks[1], cols, len(parts), piece),
        (*parts, w_query, w_output, wkv, out_sum, grad_sum),
        [VMEM] * (len(parts) + 5),
        [piece_half] * 2,
        [VMEM] * 2,
        [pltpu.VMEM((rows, features), F32), pltpu.VMEM((rows, features), F32)],
        8 * MIB,
        rows * weight_size,
        weight_size,
    )
    far = swap(far, "narrow", narrow, 1)
    sums = call(
        add_pieces_kernel,
        (near, far),
        [VMEM] * 2,
        [piece_pair] * (narrow // 2),
        [VMEM] * (narrow // 2),
        [],
        2 * MIB,
        2 * rows * features,
        12 * rows * features,
    )
    sums = [sums[0]] + [swap(sums[i], "narrow", narrow, 2 * i) for i in range(1, narrow // 2)]
    blocks = blocks[0] + blocks[1]
    ins = (turned, *grad_pieces, *parts, *grads)
    grad_wq, grad_wo, grad_wkv = call(
        functools.partial(weight_grad_kernel, blocks, cols, narrow, len(parts)),
        ins,
        [VMEM] * (1 + narrow + len(parts)) + [ANY] * 2,
        grad_shapes + [jax.ShapeDtypeStruct(w_keyval.shape, BF)],
        [ANY] * 3,
        [pltpu.VMEM(w_keyval.shape, BF)] + grad_scratch(blocks),
        20 * MIB,
        8 * rows * features * cols * len(blocks),
        8 * features * cols * len(blocks),
        {len(ins) - 2: 0, len(ins) - 1: 1},
    )
    output, grad_tokens = call(
        finish_kernel,
        sums,
        [VMEM] * len(sums),
        [piece_shape] * 2,
        [VMEM] * 2,
        [],
        4 * MIB,
        2 * narrow * piece * features,
        4 * narrow * piece * features,
    )
    return (output, grad_tokens, grad_wq, grad_wkv, grad_wo)


def solution(mesh):
    return jax.shard_map(
        functools.partial(shards, mesh.shape["narrow"], mesh.shape["wide"]),
        mesh=mesh,
        in_specs=(
            P("narrow", "wide"),
            P("wide", "narrow"),
            P("wide", "narrow"),
            P("narrow", "wide"),
            P("narrow", "wide"),
        ),
        out_specs=(
            P("narrow", "wide"),
            P("narrow", "wide"),
            P("wide", "narrow"),
            P("wide", "narrow"),
            P("narrow", "wide"),
        ),
        check_vma=False,
    )
```

```python
import functools

import jax
import jax.numpy as jnp
from jax import lax
from jax.experimental import pallas as pl
from jax.experimental.pallas import tpu as pltpu
from jax.sharding import PartitionSpec as P

HD = 128


def contract_rows(left, right):
    return lax.dot_general(
        left, right, (((0,), (0,)), ((), ())), preferred_element_type=jnp.float32
    )


def contract_cols(left, right):
    return lax.dot_general(
        left, right, (((1,), (1,)), ((), ())), preferred_element_type=jnp.float32
    )


def wide_sum(term_fn, all_rows):
    return lax.psum_scatter(
        term_fn(jnp.int32(0), lax.axis_size("wide") * (all_rows // lax.axis_size("wide"))),
        "wide",
        scatter_dimension=0,
        tiled=True,
    )


def row_shards(tokens, w_query, w_keyval, w_output, grad_out):
    wide_index = lax.axis_index("wide")
    token_panel = lax.all_gather(tokens, "narrow", axis=0, tiled=True)
    all_rows = token_panel.shape[0]
    query_cols = w_query.shape[1]
    pair_cols = w_keyval.shape[1]
    joined = jnp.concatenate([w_query, w_keyval], axis=1)

    def project_all(first_row, row_count):
        return jnp.dot(token_panel, joined, preferred_element_type=jnp.float32)

    projected = wide_sum(project_all, all_rows)
    queries = projected[:, :query_cols].astype(jnp.bfloat16)
    kv_own = projected[:, query_cols:].astype(jnp.bfloat16)
    kv_panel = lax.all_gather(kv_own, "wide", axis=0, tiled=True)
    rows_here = queries.shape[0]
    heads_here = query_cols // HD
    groups_here = pair_cols // (2 * HD)
    group_size = heads_here // groups_here
    score_scale = HD ** (-0.5)
    query_pos = wide_index * rows_here + lax.iota(jnp.int32, rows_here)
    key_pos = lax.iota(jnp.int32, all_rows)
    allowed = key_pos[None, :] <= query_pos[:, None]
    query_heads = queries.reshape(rows_here, groups_here, group_size, HD)
    pair_heads = kv_panel.reshape(all_rows, groups_here, 2, HD)
    key_heads = pair_heads[:, :, 0]
    value_heads = pair_heads[:, :, 1]
    scores = (
        jnp.einsum("rghd,sgd->ghrs", query_heads, key_heads, preferred_element_type=jnp.float32)
        * score_scale
    )
    weights = jnp.where(allowed, jnp.exp(scores), 0.0)
    weights = weights / jnp.sum(weights, axis=3, keepdims=True)
    prob_bf = weights.astype(jnp.bfloat16)
    attended = jnp.einsum(
        "ghrs,sgd->rghd", prob_bf, value_heads, preferred_element_type=jnp.float32
    )
    attended = attended.reshape(rows_here, query_cols).astype(jnp.bfloat16)
    att_panel = lax.all_gather(attended, "wide", axis=0, tiled=True)
    row_block = att_panel
    output = lax.psum_scatter(
        jnp.dot(row_block, w_output, preferred_element_type=jnp.float32).astype(jnp.bfloat16),
        "narrow",
        scatter_dimension=0,
        tiled=True,
    )
    grad_panel = lax.all_gather(grad_out, "narrow", axis=0, tiled=True)
    grad_wo = contract_rows(att_panel, grad_panel).astype(jnp.bfloat16)

    def back_out(first_row, row_count):
        return contract_cols(grad_panel, w_output)

    grad_att = wide_sum(back_out, all_rows).astype(jnp.bfloat16)
    grad_heads = grad_att.reshape(rows_here, groups_here, group_size, HD)
    prob_grad = jnp.einsum(
        "rghd,sgd->ghrs", grad_heads, value_heads, preferred_element_type=jnp.float32
    )
    grad_values = jnp.einsum(
        "ghrs,rghd->sgd", prob_bf, grad_heads, preferred_element_type=jnp.float32
    )
    score_grad = weights * (prob_grad - jnp.sum(weights * prob_grad, axis=3, keepdims=True))
    score_half = score_grad.astype(jnp.bfloat16)
    grad_q = (
        jnp.einsum("ghrs,sgd->rghd", score_half, key_heads, preferred_element_type=jnp.float32)
        * score_scale
    )
    grad_q = grad_q.reshape(rows_here, query_cols).astype(jnp.bfloat16)
    grad_keys = (
        jnp.einsum("ghrs,rghd->sgd", score_half, query_heads, preferred_element_type=jnp.float32)
        * score_scale
    )
    kv_grad = jnp.stack([grad_keys, grad_values], axis=2).reshape(all_rows, pair_cols)
    kv_share = lax.psum_scatter(kv_grad, "wide", scatter_dimension=0, tiled=True).astype(
        jnp.bfloat16
    )
    grad_mixed = jnp.concatenate([grad_q, kv_share], axis=1)
    grad_rows = lax.all_gather(grad_mixed, "wide", axis=0, tiled=True)
    grad_joined = contract_rows(token_panel, grad_rows)
    grad_wq = grad_joined[:, :query_cols].astype(jnp.bfloat16)
    grad_wkv = grad_joined[:, query_cols:].astype(jnp.bfloat16)
    row_block = grad_rows
    grad_tokens = lax.psum_scatter(
        contract_cols(row_block, joined).astype(jnp.bfloat16),
        "narrow",
        scatter_dimension=0,
        tiled=True,
    )
    return (output, grad_tokens, grad_wq, grad_wkv, grad_wo)


MIB = 1 << 20
BF = jnp.bfloat16
F32 = jnp.float32
VMEM = pl.BlockSpec(memory_space=pltpu.VMEM)
ANY = pl.BlockSpec(memory_space=pl.ANY)
HBM = pl.BlockSpec(memory_space=pltpu.HBM)


def swap(value, axis, size, distance):
    return lax.ppermute(value, axis, [(i, i ^ distance) for i in range(size)])


def call(kernel, ins, in_specs, outs, out_specs, scratch, vmem, flops, moved, aliases={}):
    return pl.pallas_call(
        kernel,
        out_shape=outs,
        in_specs=in_specs,
        out_specs=out_specs,
        scratch_shapes=scratch,
        input_output_aliases=aliases,
        compiler_params=pltpu.CompilerParams(vmem_limit_bytes=vmem),
        cost_estimate=pl.CostEstimate(flops=flops, bytes_accessed=moved, transcendentals=0),
    )(*ins)


def block_of(distance, cols):
    return pl.ds(pl.multiple_of((lax.axis_index("wide") ^ distance) * cols, cols), cols)


def load_kernel(source, wq, wo, out, sem):
    copy = pltpu.make_async_copy(source, out, sem)
    copy.start()
    copy.wait()


def panels(refs):
    half = len(refs) // 2
    return (jnp.concatenate([r[...] for r in part], axis=0) for part in (refs[:half], refs[half:]))


def query_block(wq, b, cols):
    return wq[:, block_of(b, cols)]


def output_block(wo, b, cols):
    return wo[block_of(b, cols), :]


def project_blocks(token_panel, grad_panel, blocks, wq, wo, width, out):
    cols = width // (2 * len(blocks))
    for at, b in enumerate(blocks):
        left = 2 * at * cols
        out[:, left : left + cols] = jnp.dot(token_panel, query_block(wq, b, cols), preferred_element_type=F32).astype(BF)
        out[:, left + cols : left + 2 * cols] = contract_cols(grad_panel, output_block(wo, b, cols)).astype(BF)


def query_columns(panel, blocks, wq, out):
    cols = out.shape[1] // len(blocks)
    for at, b in enumerate(blocks):
        out[:, at * cols : (at + 1) * cols] = jnp.dot(panel, query_block(wq, b, cols), preferred_element_type=F32).astype(BF)


def project_first_kernel(blocks, count, *refs):
    pieces, (wq, wkv, out, kv) = refs[:count], refs[count:]
    panel = jnp.concatenate([r[...] for r in pieces], axis=0)
    kv[...] = jnp.dot(panel, wkv[...], preferred_element_type=F32).astype(BF)
    query_columns(panel, blocks, wq, out)


def project_query_kernel(blocks, count, *refs):
    pieces, (wq, out) = refs[:count], refs[count:]
    query_columns(jnp.concatenate([r[...] for r in pieces], axis=0), blocks, wq, out)


def join_block_kernel(b, at, count, *refs):
    pieces, (wo, queries, *kv, out) = refs[:count], refs[count:]
    cols = wo.shape[0] // lax.axis_size("wide")
    out[:, :cols] = queries[:, at * cols : (at + 1) * cols]
    panel = jnp.concatenate([r[...] for r in pieces], axis=0)
    out[:, cols : 2 * cols] = contract_cols(panel, output_block(wo, b, cols)).astype(BF)
    if kv:
        out[:, 2 * cols :] = kv[0][...]


def project_kernel(blocks, count, *refs):
    pieces, (wq, wo, out) = refs[:count], refs[count:]
    token_panel, grad_panel = panels(pieces)
    project_blocks(token_panel, grad_panel, blocks, wq, wo, out.shape[1], out)


def turn_kernel(*refs):
    refs[-1][...] = jnp.concatenate([r[...] for r in refs[:-1]], axis=0).T


def plus(left, right):
    return left.astype(F32) + right.astype(F32)


def total(parts):
    value = parts[0][...].astype(F32)
    for part in parts[1:]:
        value = value + part[...].astype(F32)
    return value


def add_first_kernel(near, kv, far, out, pair):
    width = near.shape[1]
    out[:, :width] = plus(near[...], far[:, :width]).astype(BF)
    pair[...] = plus(kv[...], far[:, width:]).astype(BF)
    out[:, width:] = pair[...]


def add_next_kernel(near, far, pair, out):
    width = near.shape[1]
    out[:, :width] = plus(near[...], far[...]).astype(BF)
    out[:, width:] = pair[...]


def attend_kernel(narrow, near, far, pair, *refs):
    parts, out = refs[:-1], refs[-1]
    value = jnp.concatenate([plus(near[...], far[...]), pair[...].astype(F32)], axis=1)
    value = (value + total(parts)).astype(BF)
    rows = value.shape[0]
    cols = (value.shape[1] - 2 * HD) // 2
    piece = rows // narrow
    me = lax.axis_index("narrow")

    def position(dim):
        at = lax.broadcasted_iota(jnp.int32, (rows, rows), dim)
        return ((at // piece) ^ me) * piece + at % piece

    allowed = position(1) <= position(0)
    keys, values = value[:, 2 * cols : 2 * cols + HD], value[:, 2 * cols + HD :]
    scale = HD ** (-0.5)
    grad_keys = jnp.zeros((rows, HD), F32)
    grad_values = jnp.zeros((rows, HD), F32)
    for at in range(0, cols, HD):
        queries, grads = value[:, at : at + HD], value[:, cols + at : cols + at + HD]
        weights = jnp.where(allowed, jnp.exp(contract_cols(queries, keys) * scale), 0.0)
        weights = weights / jnp.sum(weights, axis=1, keepdims=True)
        probs = weights.astype(BF)
        out[:, at : at + HD] = jnp.dot(probs, values, preferred_element_type=F32).astype(BF)
        prob_grad = contract_cols(grads, values)
        score_grad = weights * (prob_grad - jnp.sum(weights * prob_grad, axis=1, keepdims=True))
        score_half = score_grad.astype(BF)
        out[:, cols + at : cols + at + HD] = (
            jnp.dot(score_half, keys, preferred_element_type=F32) * scale
        ).astype(BF)
        grad_keys = grad_keys + contract_rows(score_half, queries) * scale
        grad_values = grad_values + contract_rows(probs, grads)
    out[:, 2 * cols : 2 * cols + HD] = grad_keys.astype(BF)
    out[:, 2 * cols + HD :] = grad_values.astype(BF)


def join_kernel(width, *refs):
    parts, out = refs[:-1], refs[-1]
    kv = parts[0][:, width:].astype(F32)
    for at, part in enumerate(parts):
        out[:, at * width : (at + 1) * width] = part[:, :width]
        if at:
            kv = kv + part[:, width:].astype(F32)
    out[:, len(parts) * width :] = kv.astype(BF)


def accumulate(blocks, cols, parts, wq, wo, before, out_sum, grad_sum):
    for i, (part, left, b) in enumerate(blocks):
        out = jnp.dot(parts[part][:, left : left + cols], output_block(wo, b, cols), preferred_element_type=F32)
        grad = contract_cols(parts[part][:, left + cols : left + 2 * cols], query_block(wq, b, cols))
        if i == 0 and before:
            out, grad = out + before[0][...], grad + before[1][...]
        elif i:
            out, grad = out + out_sum[...], grad + grad_sum[...]
        out_sum[...] = out
        grad_sum[...] = grad


def back_kernel(blocks, cols, count, *refs):
    parts, (wq, wo), rest = refs[:count], refs[count : count + 2], refs[count + 2 :]
    accumulate(blocks, cols, parts, wq, wo, rest[:-2], *rest[-2:])


def kv_total(parts):
    total = parts[0][:, parts[0].shape[1] - 2 * HD :].astype(F32)
    for part in parts[1:]:
        total = total + part[:, part.shape[1] - 2 * HD :].astype(F32)
    return total.astype(BF)


def back_last_kernel(blocks, cols, count, piece, *refs):
    parts, (wq, wo, wkv, out_before, grad_before, near, far, out_sum, grad_sum) = refs[:count], refs[count:]
    accumulate(blocks, cols, parts, wq, wo, (out_before, grad_before), out_sum, grad_sum)
    grad_sum[...] += contract_cols(kv_total(parts), wkv[...])
    for out, low in ((near, 0), (far, 1)):
        for at in range(out.shape[0] // (2 * piece)):
            first = (2 * at + low) * piece
            out[2 * at * piece : (2 * at + 1) * piece, :] = out_sum[first : first + piece, :].astype(BF)
            out[(2 * at + 1) * piece : (2 * at + 2) * piece, :] = grad_sum[first : first + piece, :].astype(BF)


def send_weight_grads(blocks, cols, turned, grads, parts, gwq, gwo, gwq_v, gwo_v, sems):
    grad_panel = jnp.concatenate([r[...] for r in grads], axis=0)
    copies = []

    def send(source, target):
        copies.append(pltpu.make_async_copy(source, target, sems.at[len(copies)]))
        copies[-1].start()

    tile = 256
    for at, (part, left, b) in enumerate(blocks):
        att = parts[part][:, left : left + cols].T
        for first in range(0, gwo.shape[1], tile):
            span = slice(first, first + tile)
            gwo_v[at, :, span] = jnp.dot(att, grad_panel[:, span], preferred_element_type=F32).astype(BF)
        send(gwo_v.at[at], gwo.at[block_of(b, cols), :])
        grad = parts[part][:, left + cols : left + 2 * cols]
        for first in range(0, gwq.shape[0], tile):
            span = slice(first, first + tile)
            gwq_v[at, span, :] = jnp.dot(turned[span, :], grad, preferred_element_type=F32).astype(BF)
        send(gwq_v.at[at], gwq.at[:, block_of(b, cols)])
    return copies


def block_kernel(blocks, cols, narrow, count, has_before, *refs):
    turned, grads, parts, refs = refs[0], refs[1 : 1 + narrow], refs[1 + narrow : 1 + narrow + count], refs[1 + narrow + count :]
    wq, wo = refs[:2]
    before, outs = (refs[2:4], refs[6:]) if has_before else ((), refs[2:])
    gwq, gwo, out_sum, grad_sum, gwq_v, gwo_v, sems = outs
    copies = send_weight_grads(blocks, cols, turned, grads, parts, gwq, gwo, gwq_v, gwo_v, sems)
    accumulate(blocks, cols, parts, wq, wo, before, out_sum, grad_sum)
    for copy in copies:
        copy.wait()


def weight_grad_kernel(blocks, cols, narrow, count, *refs):
    turned, grads, parts = refs[0], refs[1 : 1 + narrow], refs[1 + narrow : 1 + narrow + count]
    gwq, gwo, gwkv, gwkv_v, gwq_v, gwo_v, sems = refs[3 + narrow + count :]
    gwkv_v[...] = jnp.dot(turned[...], kv_total(parts), preferred_element_type=F32).astype(BF)
    last = pltpu.make_async_copy(gwkv_v, gwkv, sems.at[2 * len(blocks)])
    last.start()
    copies = send_weight_grads(blocks, cols, turned, grads, parts, gwq, gwo, gwq_v, gwo_v, sems)
    for copy in copies + [last]:
        copy.wait()


def add_pieces_kernel(near, far, own, *outs):
    rows = own.shape[0]
    for at, out in enumerate((own,) + outs):
        part = slice(at * rows, (at + 1) * rows)
        out[...] = plus(near[part, :], far[part, :]).astype(BF)


def finish_kernel(*refs):
    parts, output, grad = refs[:-2], refs[-2], refs[-1]
    value = total(parts)
    rows = output.shape[0]
    output[...] = value[:rows].astype(BF)
    grad[...] = value[rows:].astype(BF)


def shards(narrow, wide, tokens, w_query, w_keyval, w_output, grad_out):
    piece, features = tokens.shape
    query_cols, pair_cols = w_query.shape[1], w_keyval.shape[1]
    cols = query_cols // wide
    if pair_cols != 2 * HD or cols % HD or cols * wide != query_cols or piece % 16 or narrow & (narrow - 1) or wide & (wide - 1) or wide < 8 or narrow < 2:
        return row_shards(tokens, w_query, w_keyval, w_output, grad_out)
    rows = narrow * piece
    weight_size = features * (2 * query_cols + pair_cols)
    full = jax.ShapeDtypeStruct((rows, 2 * cols + pair_cols), BF)
    piece_shape = jax.ShapeDtypeStruct((piece, features), BF)
    half = wide // 2
    sems = pltpu.SemaphoreType.DMA((4 * wide,))

    def spread(value):
        pieces = {0: value}
        bit = narrow // 2
        while bit > 1:
            pieces.update({b ^ bit: swap(p, "narrow", narrow, bit) for b, p in pieces.items()})
            bit //= 2
        return {b: p for b, p in pieces.items() if b}

    token_pieces, grad_pieces = spread(tokens), spread(grad_out)
    beside = [{0: v, 1: swap(v, "narrow", narrow, 1)} for v in (tokens, grad_out)]
    near_blocks = list(range(wide - 2, -1, -2))
    near_blocks[:2] = near_blocks[1::-1]
    far_blocks = [b + 1 for b in near_blocks]
    wkv = call(
        load_kernel,
        [pltpu.with_memory_space_constraint(w, pltpu.HBM) for w in (w_keyval, w_query, w_output)],
        [HBM] * 3,
        jax.ShapeDtypeStruct(w_keyval.shape, BF),
        VMEM,
        [pltpu.SemaphoreType.DMA],
        2 * MIB,
        0,
        2 * weight_size,
    )
    def complete(pieces, own, behind):
        pieces, _ = lax.optimization_barrier((pieces, behind))
        pieces = {**own, **pieces}
        pieces.update({b ^ 1: swap(p, "narrow", narrow, 1) for b, p in pieces.items() if b > 1})
        return [pieces[b] for b in range(narrow)]

    token_pieces = complete(token_pieces, beside[0], wkv)
    kv_shape = jax.ShapeDtypeStruct((rows, pair_cols), BF)
    query_first, kv = call(
        functools.partial(project_first_kernel, far_blocks[:1], narrow),
        (*token_pieces, w_query, wkv),
        [VMEM] * (narrow + 2),
        [jax.ShapeDtypeStruct((rows, cols), BF), kv_shape],
        [VMEM] * 2,
        [],
        8 * MIB,
        2 * rows * features * (cols + pair_cols),
        2 * features * (cols + pair_cols),
    )
    grad_pieces = complete(grad_pieces, beside[1], wkv)
    query_rest = call(
        functools.partial(project_query_kernel, far_blocks[1:], narrow),
        (*token_pieces, w_query),
        [VMEM] * (narrow + 1),
        jax.ShapeDtypeStruct((rows, cols * (half - 1)), BF),
        VMEM,
        [],
        8 * MIB,
        2 * rows * features * cols * (half - 1),
        2 * features * cols * (half - 1),
    )
    most = half - 1
    pieces = (*token_pieces, *grad_pieces)
    count = 2 * narrow

    def project(block, pieces=pieces):
        return call(
            functools.partial(project_kernel, [block], count),
            (*pieces, w_query, w_output),
            [VMEM] * (count + 2),
            jax.ShapeDtypeStruct((rows, 2 * cols), BF),
            VMEM,
            [],
            8 * MIB,
            4 * rows * features * cols,
            4 * features * cols,
        )

    def far_swap(at):
        queries = (query_rest,) if at else (query_first, kv)
        block = call(
            functools.partial(join_block_kernel, far_blocks[at], max(at - 1, 0), narrow),
            (*grad_pieces, w_output, *queries),
            [VMEM] * (narrow + 1 + len(queries)),
            jax.ShapeDtypeStruct((rows, 2 * cols + (0 if at else pair_cols)), BF),
            VMEM,
            [],
            8 * MIB,
            2 * rows * features * cols,
            2 * features * cols,
        )
        return swap(block, "wide", wide, 1)

    far = [far_swap(at) for at in range(most)]
    sums, pair = [], None
    for at in range(most):
        near = project(near_blocks[at])
        added, *rest = call(
            add_next_kernel if sums else add_first_kernel,
            (near, far[at], pair) if sums else (near, kv, far[at]),
            [VMEM] * 3,
            [full] if sums else [full, jax.ShapeDtypeStruct((rows, pair_cols), BF)],
            [VMEM] * (1 if sums else 2),
            [],
            2 * MIB,
            rows * 1024,
            rows * 4096,
        )
        pair = rest[0] if rest else pair
        sums.append(added)
    received = [swap(part, "wide", wide, d) for part, d in zip(sums, near_blocks)]
    far_last = far_swap(most)
    later, _ = lax.optimization_barrier((pieces, sums[-1]))
    near_last = project(near_blocks[most], later)
    turned = call(
        turn_kernel,
        later[:narrow],
        [VMEM] * narrow,
        jax.ShapeDtypeStruct((features, rows), BF),
        VMEM,
        [],
        2 * MIB,
        0,
        4 * rows * features,
    )
    near_last, turned = lax.optimization_barrier((near_last, turned))
    own = call(
        functools.partial(attend_kernel, narrow),
        (near_last, far_last, pair, *received),
        [VMEM] * (3 + len(received)),
        full,
        VMEM,
        [],
        4 * MIB,
        24 * rows * rows * cols,
        2 * rows * wide * full.shape[1],
    )
    width = 2 * cols
    width = 2 * cols
    sum_shapes = [jax.ShapeDtypeStruct((rows, features), F32)] * 2
    grad_shapes = [jax.ShapeDtypeStruct(w.shape, BF) for w in (w_query, w_output)]

    def grad_scratch(blocks):
        return [pltpu.VMEM((len(blocks), features, cols), BF), pltpu.VMEM((len(blocks), cols, features), BF), sems]

    def block_terms(distances, before=()):
        blocks = [(i, 0, d) for i, d in enumerate(distances)]
        ins = (turned, *grad_pieces, *[same[d] for d in distances], w_query, w_output, *before)
        return call(
            functools.partial(block_kernel, blocks, cols, narrow, len(blocks), bool(before)),
            ins,
            [VMEM] * (3 + narrow + len(blocks)) + ([VMEM] * 2 + [ANY] * 2 if before else []),
            grad_shapes + sum_shapes,
            [ANY] * 2 + [VMEM] * 2,
            grad_scratch(blocks),
            20 * MIB,
            8 * rows * features * cols * len(blocks),
            8 * features * cols * len(blocks),
            {len(ins) - 2: 0, len(ins) - 1: 1} if before else {},
        )

    same = {0: own, **{d: swap(own, "wide", wide, d) for d in range(wide - 2, 0, -2)}}
    first, rest = 2, list(range(wide - 2, 2, -2))
    groups = ([0, first], rest)
    joined = []
    for group in groups:
        if joined:
            *grads, out_sum, grad_sum = block_terms([0, first])
            same[rest[-1]], grads, out_sum, grad_sum = lax.optimization_barrier((same[rest[-1]], grads, out_sum, grad_sum))
        together = call(
            functools.partial(join_kernel, width),
            [same[d] for d in group],
            [VMEM] * len(group),
            jax.ShapeDtypeStruct((rows, width * len(group) + pair_cols), BF),
            VMEM,
            [],
            2 * MIB,
            0,
            4 * rows * full.shape[1] * len(group),
        )
        joined.append(swap(together, "wide", wide, 1))
    *grads, out_sum, grad_sum = block_terms(rest, (out_sum, grad_sum, *grads))
    blocks = [[(i, width * at, d + 1) for at, d in enumerate(group)] for i, group in enumerate(groups)]
    out_sum, grad_sum = call(
        functools.partial(back_kernel, blocks[0], cols, 1),
        (joined[0], w_query, w_output, out_sum, grad_sum),
        [VMEM] * 5,
        sum_shapes,
        [VMEM] * 2,
        [],
        8 * MIB,
        4 * rows * features * cols * len(blocks[0]),
        4 * features * cols * len(blocks[0]),
    )
    parts = [*joined, *same.values()]
    piece_half = jax.ShapeDtypeStruct((narrow * piece, features), BF)
    piece_pair = jax.ShapeDtypeStruct((2 * piece, features), BF)
    near, far = call(
        functools.partial(back_last_kernel, blocks[1], cols, len(parts), piece),
        (*parts, w_query, w_output, wkv, out_sum, grad_sum),
        [VMEM] * (len(parts) + 5),
        [piece_half] * 2,
        [VMEM] * 2,
        [pltpu.VMEM((rows, features), F32), pltpu.VMEM((rows, features), F32)],
        8 * MIB,
        rows * weight_size,
        weight_size,
    )
    far = swap(far, "narrow", narrow, 1)
    sums = call(
        add_pieces_kernel,
        (near, far),
        [VMEM] * 2,
        [piece_pair] * (narrow // 2),
        [VMEM] * (narrow // 2),
        [],
        2 * MIB,
        2 * rows * features,
        12 * rows * features,
    )
    sums = [sums[0]] + [swap(sums[i], "narrow", narrow, 2 * i) for i in range(1, narrow // 2)]
    blocks = blocks[0] + blocks[1]
    ins = (turned, *grad_pieces, *parts, *grads)
    grad_wq, grad_wo, grad_wkv = call(
        functools.partial(weight_grad_kernel, blocks, cols, narrow, len(parts)),
        ins,
        [VMEM] * (1 + narrow + len(parts)) + [ANY] * 2,
        grad_shapes + [jax.ShapeDtypeStruct(w_keyval.shape, BF)],
        [ANY] * 3,
        [pltpu.VMEM(w_keyval.shape, BF)] + grad_scratch(blocks),
        20 * MIB,
        8 * rows * features * cols * len(blocks),
        8 * features * cols * len(blocks),
        {len(ins) - 2: 0, len(ins) - 1: 1},
    )
    output, grad_tokens = call(
        finish_kernel,
        sums,
        [VMEM] * len(sums),
        [piece_shape] * 2,
        [VMEM] * 2,
        [],
        4 * MIB,
        2 * narrow * piece * features,
        4 * narrow * piece * features,
    )
    return (output, grad_tokens, grad_wq, grad_wkv, grad_wo)


def solution(mesh):
    return jax.shard_map(
        functools.partial(shards, mesh.shape["narrow"], mesh.shape["wide"]),
        mesh=mesh,
        in_specs=(
            P("narrow", "wide"),
            P("wide", "narrow"),
            P("wide", "narrow"),
            P("narrow", "wide"),
            P("narrow", "wide"),
        ),
        out_specs=(
            P("narrow", "wide"),
            P("narrow", "wide"),
            P("wide", "narrow"),
            P("wide", "narrow"),
            P("narrow", "wide"),
        ),
        check_vma=False,
    )
```

```python
import functools

import jax
import jax.numpy as jnp
from jax import lax
from jax.experimental import pallas as pl
from jax.experimental.pallas import tpu as pltpu
from jax.sharding import PartitionSpec as P

HD = 128


def contract_rows(left, right):
    return lax.dot_general(
        left, right, (((0,), (0,)), ((), ())), preferred_element_type=jnp.float32
    )


def contract_cols(left, right):
    return lax.dot_general(
        left, right, (((1,), (1,)), ((), ())), preferred_element_type=jnp.float32
    )


def wide_sum(term_fn, all_rows):
    return lax.psum_scatter(
        term_fn(jnp.int32(0), lax.axis_size("wide") * (all_rows // lax.axis_size("wide"))),
        "wide",
        scatter_dimension=0,
        tiled=True,
    )


def row_shards(tokens, w_query, w_keyval, w_output, grad_out):
    wide_index = lax.axis_index("wide")
    token_panel = lax.all_gather(tokens, "narrow", axis=0, tiled=True)
    all_rows = token_panel.shape[0]
    query_cols = w_query.shape[1]
    pair_cols = w_keyval.shape[1]
    joined = jnp.concatenate([w_query, w_keyval], axis=1)

    def project_all(first_row, row_count):
        return jnp.dot(token_panel, joined, preferred_element_type=jnp.float32)

    projected = wide_sum(project_all, all_rows)
    queries = projected[:, :query_cols].astype(jnp.bfloat16)
    kv_own = projected[:, query_cols:].astype(jnp.bfloat16)
    kv_panel = lax.all_gather(kv_own, "wide", axis=0, tiled=True)
    rows_here = queries.shape[0]
    heads_here = query_cols // HD
    groups_here = pair_cols // (2 * HD)
    group_size = heads_here // groups_here
    score_scale = HD ** (-0.5)
    query_pos = wide_index * rows_here + lax.iota(jnp.int32, rows_here)
    key_pos = lax.iota(jnp.int32, all_rows)
    allowed = key_pos[None, :] <= query_pos[:, None]
    query_heads = queries.reshape(rows_here, groups_here, group_size, HD)
    pair_heads = kv_panel.reshape(all_rows, groups_here, 2, HD)
    key_heads = pair_heads[:, :, 0]
    value_heads = pair_heads[:, :, 1]
    scores = (
        jnp.einsum("rghd,sgd->ghrs", query_heads, key_heads, preferred_element_type=jnp.float32)
        * score_scale
    )
    weights = jnp.where(allowed, jnp.exp(scores), 0.0)
    weights = weights / jnp.sum(weights, axis=3, keepdims=True)
    prob_bf = weights.astype(jnp.bfloat16)
    attended = jnp.einsum(
        "ghrs,sgd->rghd", prob_bf, value_heads, preferred_element_type=jnp.float32
    )
    attended = attended.reshape(rows_here, query_cols).astype(jnp.bfloat16)
    att_panel = lax.all_gather(attended, "wide", axis=0, tiled=True)
    row_block = att_panel
    output = lax.psum_scatter(
        jnp.dot(row_block, w_output, preferred_element_type=jnp.float32).astype(jnp.bfloat16),
        "narrow",
        scatter_dimension=0,
        tiled=True,
    )
    grad_panel = lax.all_gather(grad_out, "narrow", axis=0, tiled=True)
    grad_wo = contract_rows(att_panel, grad_panel).astype(jnp.bfloat16)

    def back_out(first_row, row_count):
        return contract_cols(grad_panel, w_output)

    grad_att = wide_sum(back_out, all_rows).astype(jnp.bfloat16)
    grad_heads = grad_att.reshape(rows_here, groups_here, group_size, HD)
    prob_grad = jnp.einsum(
        "rghd,sgd->ghrs", grad_heads, value_heads, preferred_element_type=jnp.float32
    )
    grad_values = jnp.einsum(
        "ghrs,rghd->sgd", prob_bf, grad_heads, preferred_element_type=jnp.float32
    )
    score_grad = weights * (prob_grad - jnp.sum(weights * prob_grad, axis=3, keepdims=True))
    score_half = score_grad.astype(jnp.bfloat16)
    grad_q = (
        jnp.einsum("ghrs,sgd->rghd", score_half, key_heads, preferred_element_type=jnp.float32)
        * score_scale
    )
    grad_q = grad_q.reshape(rows_here, query_cols).astype(jnp.bfloat16)
    grad_keys = (
        jnp.einsum("ghrs,rghd->sgd", score_half, query_heads, preferred_element_type=jnp.float32)
        * score_scale
    )
    kv_grad = jnp.stack([grad_keys, grad_values], axis=2).reshape(all_rows, pair_cols)
    kv_share = lax.psum_scatter(kv_grad, "wide", scatter_dimension=0, tiled=True).astype(
        jnp.bfloat16
    )
    grad_mixed = jnp.concatenate([grad_q, kv_share], axis=1)
    grad_rows = lax.all_gather(grad_mixed, "wide", axis=0, tiled=True)
    grad_joined = contract_rows(token_panel, grad_rows)
    grad_wq = grad_joined[:, :query_cols].astype(jnp.bfloat16)
    grad_wkv = grad_joined[:, query_cols:].astype(jnp.bfloat16)
    row_block = grad_rows
    grad_tokens = lax.psum_scatter(
        contract_cols(row_block, joined).astype(jnp.bfloat16),
        "narrow",
        scatter_dimension=0,
        tiled=True,
    )
    return (output, grad_tokens, grad_wq, grad_wkv, grad_wo)


MIB = 1 << 20
BF = jnp.bfloat16
F32 = jnp.float32
VMEM = pl.BlockSpec(memory_space=pltpu.VMEM)
ANY = pl.BlockSpec(memory_space=pl.ANY)
HBM = pl.BlockSpec(memory_space=pltpu.HBM)


def swap(value, axis, size, distance):
    return lax.ppermute(value, axis, [(i, i ^ distance) for i in range(size)])


def call(kernel, ins, in_specs, outs, out_specs, scratch, vmem, flops, moved, aliases={}):
    return pl.pallas_call(
        kernel,
        out_shape=outs,
        in_specs=in_specs,
        out_specs=out_specs,
        scratch_shapes=scratch,
        input_output_aliases=aliases,
        compiler_params=pltpu.CompilerParams(vmem_limit_bytes=vmem),
        cost_estimate=pl.CostEstimate(flops=flops, bytes_accessed=moved, transcendentals=0),
    )(*ins)


def block_of(distance, cols):
    return pl.ds(pl.multiple_of((lax.axis_index("wide") ^ distance) * cols, cols), cols)


def load_kernel(source, wq, wo, out, sem):
    copy = pltpu.make_async_copy(source, out, sem)
    copy.start()
    copy.wait()


def panels(refs):
    half = len(refs) // 2
    return (jnp.concatenate([r[...] for r in part], axis=0) for part in (refs[:half], refs[half:]))


def query_block(wq, b, cols):
    return wq[:, block_of(b, cols)]


def output_block(wo, b, cols):
    return wo[block_of(b, cols), :]


def project_blocks(token_panel, grad_panel, blocks, wq, wo, width, out):
    cols = width // (2 * len(blocks))
    for at, b in enumerate(blocks):
        left = 2 * at * cols
        out[:, left : left + cols] = jnp.dot(token_panel, query_block(wq, b, cols), preferred_element_type=F32).astype(BF)
        out[:, left + cols : left + 2 * cols] = contract_cols(grad_panel, output_block(wo, b, cols)).astype(BF)


def query_columns(panel, blocks, wq, out):
    cols = out.shape[1] // len(blocks)
    for at, b in enumerate(blocks):
        out[:, at * cols : (at + 1) * cols] = jnp.dot(panel, query_block(wq, b, cols), preferred_element_type=F32).astype(BF)


def project_first_kernel(blocks, count, *refs):
    pieces, (wq, wkv, out, kv) = refs[:count], refs[count:]
    panel = jnp.concatenate([r[...] for r in pieces], axis=0)
    kv[...] = jnp.dot(panel, wkv[...], preferred_element_type=F32).astype(BF)
    query_columns(panel, blocks, wq, out)


def project_query_kernel(blocks, count, *refs):
    pieces, (wq, out) = refs[:count], refs[count:]
    query_columns(jnp.concatenate([r[...] for r in pieces], axis=0), blocks, wq, out)


def join_block_kernel(b, at, count, *refs):
    pieces, (wo, queries, *kv, out) = refs[:count], refs[count:]
    cols = wo.shape[0] // lax.axis_size("wide")
    out[:, :cols] = queries[:, at * cols : (at + 1) * cols]
    panel = jnp.concatenate([r[...] for r in pieces], axis=0)
    out[:, cols : 2 * cols] = contract_cols(panel, output_block(wo, b, cols)).astype(BF)
    if kv:
        out[:, 2 * cols :] = kv[0][...]


def project_kernel(blocks, count, *refs):
    pieces, (wq, wo, out) = refs[:count], refs[count:]
    token_panel, grad_panel = panels(pieces)
    project_blocks(token_panel, grad_panel, blocks, wq, wo, out.shape[1], out)


def turn_kernel(*refs):
    refs[-1][...] = jnp.concatenate([r[...] for r in refs[:-1]], axis=0).T


def plus(left, right):
    return left.astype(F32) + right.astype(F32)


def total(parts):
    value = parts[0][...].astype(F32)
    for part in parts[1:]:
        value = value + part[...].astype(F32)
    return value


def add_first_kernel(near, kv, far, out, pair):
    width = near.shape[1]
    out[:, :width] = plus(near[...], far[:, :width]).astype(BF)
    pair[...] = plus(kv[...], far[:, width:]).astype(BF)
    out[:, width:] = pair[...]


def add_next_kernel(near, far, pair, out):
    width = near.shape[1]
    out[:, :width] = plus(near[...], far[...]).astype(BF)
    out[:, width:] = pair[...]


def attend_kernel(narrow, near, far, pair, *refs):
    parts, out = refs[:-1], refs[-1]
    value = jnp.concatenate([plus(near[...], far[...]), pair[...].astype(F32)], axis=1)
    value = (value + total(parts)).astype(BF)
    rows = value.shape[0]
    cols = (value.shape[1] - 2 * HD) // 2
    piece = rows // narrow
    me = lax.axis_index("narrow")

    def position(dim):
        at = lax.broadcasted_iota(jnp.int32, (rows, rows), dim)
        return ((at // piece) ^ me) * piece + at % piece

    allowed = position(1) <= position(0)
    keys, values = value[:, 2 * cols : 2 * cols + HD], value[:, 2 * cols + HD :]
    scale = HD ** (-0.5)
    grad_keys = jnp.zeros((rows, HD), F32)
    grad_values = jnp.zeros((rows, HD), F32)
    for at in range(0, cols, HD):
        queries, grads = value[:, at : at + HD], value[:, cols + at : cols + at + HD]
        weights = jnp.where(allowed, jnp.exp(contract_cols(queries, keys) * scale), 0.0)
        weights = weights / jnp.sum(weights, axis=1, keepdims=True)
        probs = weights.astype(BF)
        out[:, at : at + HD] = jnp.dot(probs, values, preferred_element_type=F32).astype(BF)
        prob_grad = contract_cols(grads, values)
        score_grad = weights * (prob_grad - jnp.sum(weights * prob_grad, axis=1, keepdims=True))
        score_half = score_grad.astype(BF)
        out[:, cols + at : cols + at + HD] = (
            jnp.dot(score_half, keys, preferred_element_type=F32) * scale
        ).astype(BF)
        grad_keys = grad_keys + contract_rows(score_half, queries) * scale
        grad_values = grad_values + contract_rows(probs, grads)
    out[:, 2 * cols : 2 * cols + HD] = grad_keys.astype(BF)
    out[:, 2 * cols + HD :] = grad_values.astype(BF)


def join_kernel(width, *refs):
    parts, out = refs[:-1], refs[-1]
    kv = parts[0][:, width:].astype(F32)
    for at, part in enumerate(parts):
        out[:, at * width : (at + 1) * width] = part[:, :width]
        if at:
            kv = kv + part[:, width:].astype(F32)
    out[:, len(parts) * width :] = kv.astype(BF)


def accumulate(blocks, cols, parts, wq, wo, before, out_sum, grad_sum):
    for i, (part, left, b) in enumerate(blocks):
        out = jnp.dot(parts[part][:, left : left + cols], output_block(wo, b, cols), preferred_element_type=F32)
        grad = contract_cols(parts[part][:, left + cols : left + 2 * cols], query_block(wq, b, cols))
        if i == 0 and before:
            out, grad = out + before[0][...], grad + before[1][...]
        elif i:
            out, grad = out + out_sum[...], grad + grad_sum[...]
        out_sum[...] = out
        grad_sum[...] = grad


def back_kernel(blocks, cols, count, *refs):
    parts, (wq, wo), rest = refs[:count], refs[count : count + 2], refs[count + 2 :]
    accumulate(blocks, cols, parts, wq, wo, rest[:-2], *rest[-2:])


def kv_total(parts):
    total = parts[0][:, parts[0].shape[1] - 2 * HD :].astype(F32)
    for part in parts[1:]:
        total = total + part[:, part.shape[1] - 2 * HD :].astype(F32)
    return total.astype(BF)


def back_last_kernel(blocks, cols, count, piece, *refs):
    parts, (wq, wo, wkv, out_before, grad_before, near, far, out_sum, grad_sum) = refs[:count], refs[count:]
    accumulate(blocks, cols, parts, wq, wo, (out_before, grad_before), out_sum, grad_sum)
    grad_sum[...] += contract_cols(kv_total(parts), wkv[...])
    for out, low in ((near, 0), (far, 1)):
        for at in range(out.shape[0] // (2 * piece)):
            first = (2 * at + low) * piece
            out[2 * at * piece : (2 * at + 1) * piece, :] = out_sum[first : first + piece, :].astype(BF)
            out[(2 * at + 1) * piece : (2 * at + 2) * piece, :] = grad_sum[first : first + piece, :].astype(BF)


def send_weight_grads(blocks, cols, turned, grads, parts, gwq, gwo, gwq_v, gwo_v, sems):
    grad_panel = jnp.concatenate([r[...] for r in grads], axis=0)
    copies = []

    def send(source, target):
        copies.append(pltpu.make_async_copy(source, target, sems.at[len(copies)]))
        copies[-1].start()

    tile = 256
    for at, (part, left, b) in enumerate(blocks):
        att = parts[part][:, left : left + cols].T
        half = cols // 2
        for top in (0, half):
            for first in range(0, gwo.shape[1], tile):
                span = slice(first, first + tile)
                gwo_v[at, top : top + half, span] = jnp.dot(
                    att[top : top + half, :], grad_panel[:, span], preferred_element_type=F32
                ).astype(BF)
            me = lax.axis_index("wide") ^ b
            rows = pl.ds(pl.multiple_of(me * cols + top, half), half)
            send(gwo_v.at[at, pl.ds(top, half), :], gwo.at[rows, :])
        grad = parts[part][:, left + cols : left + 2 * cols]
        half = gwq.shape[0] // 2
        for top in (0, half):
            for first in range(top, top + half, tile):
                span = slice(first, first + tile)
                gwq_v[at, span, :] = jnp.dot(turned[span, :], grad, preferred_element_type=F32).astype(BF)
            send(gwq_v.at[at, pl.ds(top, half), :], gwq.at[pl.ds(top, half), block_of(b, cols)])
    return copies


def block_kernel(blocks, written, cols, narrow, count, has_before, *refs):
    turned, grads, parts, refs = refs[0], refs[1 : 1 + narrow], refs[1 + narrow : 1 + narrow + count], refs[1 + narrow + count :]
    wq, wo = refs[:2]
    before, outs = (refs[2:4], refs[6:]) if has_before else ((), refs[2:])
    gwq, gwo, out_sum, grad_sum, gwq_v, gwo_v, sems = outs
    copies = send_weight_grads(blocks + written, cols, turned, grads, parts, gwq, gwo, gwq_v, gwo_v, sems)
    accumulate(blocks, cols, parts, wq, wo, before, out_sum, grad_sum)
    for copy in copies:
        copy.wait()


def weight_grad_kernel(blocks, cols, narrow, count, *refs):
    turned, grads, parts = refs[0], refs[1 : 1 + narrow], refs[1 + narrow : 1 + narrow + count]
    gwq, gwo, gwkv, gwkv_v, gwq_v, gwo_v, sems = refs[3 + narrow + count :]
    copies = send_weight_grads(blocks, cols, turned, grads, parts, gwq, gwo, gwq_v, gwo_v, sems)
    gwkv_v[...] = jnp.dot(turned[...], kv_total(parts), preferred_element_type=F32).astype(BF)
    last = pltpu.make_async_copy(gwkv_v, gwkv, sems.at[len(copies)])
    last.start()
    for copy in copies + [last]:
        copy.wait()


def add_pieces_kernel(near, far, own, *outs):
    rows = own.shape[0]
    for at, out in enumerate((own,) + outs):
        part = slice(at * rows, (at + 1) * rows)
        out[...] = plus(near[part, :], far[part, :]).astype(BF)


def finish_kernel(*refs):
    parts, output, grad = refs[:-2], refs[-2], refs[-1]
    value = total(parts)
    rows = output.shape[0]
    output[...] = value[:rows].astype(BF)
    grad[...] = value[rows:].astype(BF)


def shards(narrow, wide, tokens, w_query, w_keyval, w_output, grad_out):
    piece, features = tokens.shape
    query_cols, pair_cols = w_query.shape[1], w_keyval.shape[1]
    cols = query_cols // wide
    if pair_cols != 2 * HD or cols % HD or cols * wide != query_cols or piece % 16 or narrow & (narrow - 1) or wide & (wide - 1) or wide < 8 or narrow < 2:
        return row_shards(tokens, w_query, w_keyval, w_output, grad_out)
    rows = narrow * piece
    weight_size = features * (2 * query_cols + pair_cols)
    full = jax.ShapeDtypeStruct((rows, 2 * cols + pair_cols), BF)
    piece_shape = jax.ShapeDtypeStruct((piece, features), BF)
    half = wide // 2
    sems = pltpu.SemaphoreType.DMA((4 * wide,))

    def spread(value):
        pieces = {0: value}
        bit = narrow // 2
        while bit > 1:
            pieces.update({b ^ bit: swap(p, "narrow", narrow, bit) for b, p in pieces.items()})
            bit //= 2
        return {b: p for b, p in pieces.items() if b}

    token_pieces, grad_pieces = spread(tokens), spread(grad_out)
    beside = [{0: v, 1: swap(v, "narrow", narrow, 1)} for v in (tokens, grad_out)]
    far_blocks = list(range(wide - 1, 0, -2))
    near_blocks = list(range(wide - 2, -1, -2))
    wkv = call(
        load_kernel,
        [pltpu.with_memory_space_constraint(w, pltpu.HBM) for w in (w_keyval, w_query, w_output)],
        [HBM] * 3,
        jax.ShapeDtypeStruct(w_keyval.shape, BF),
        VMEM,
        [pltpu.SemaphoreType.DMA],
        2 * MIB,
        0,
        2 * weight_size,
    )
    def complete(pieces, own, behind):
        pieces, _ = lax.optimization_barrier((pieces, behind))
        pieces = {**own, **pieces}
        pieces.update({b ^ 1: swap(p, "narrow", narrow, 1) for b, p in pieces.items() if b > 1})
        return [pieces[b] for b in range(narrow)]

    token_pieces = complete(token_pieces, beside[0], wkv)
    kv_shape = jax.ShapeDtypeStruct((rows, pair_cols), BF)
    query_first, kv = call(
        functools.partial(project_first_kernel, far_blocks[:1], narrow),
        (*token_pieces, w_query, wkv),
        [VMEM] * (narrow + 2),
        [jax.ShapeDtypeStruct((rows, cols), BF), kv_shape],
        [VMEM] * 2,
        [],
        8 * MIB,
        2 * rows * features * (cols + pair_cols),
        2 * features * (cols + pair_cols),
    )
    grad_pieces = complete(grad_pieces, beside[1], wkv)
    query_rest = call(
        functools.partial(project_query_kernel, far_blocks[1:], narrow),
        (*token_pieces, w_query),
        [VMEM] * (narrow + 1),
        jax.ShapeDtypeStruct((rows, cols * (half - 1)), BF),
        VMEM,
        [],
        8 * MIB,
        2 * rows * features * cols * (half - 1),
        2 * features * cols * (half - 1),
    )
    most = half - 1
    pieces = (*token_pieces, *grad_pieces)
    count = 2 * narrow

    def project(block, pieces=pieces):
        return call(
            functools.partial(project_kernel, [block], count),
            (*pieces, w_query, w_output),
            [VMEM] * (count + 2),
            jax.ShapeDtypeStruct((rows, 2 * cols), BF),
            VMEM,
            [],
            8 * MIB,
            4 * rows * features * cols,
            4 * features * cols,
        )

    def far_swap(at):
        queries = (query_rest,) if at else (query_first, kv)
        block = call(
            functools.partial(join_block_kernel, far_blocks[at], max(at - 1, 0), narrow),
            (*grad_pieces, w_output, *queries),
            [VMEM] * (narrow + 1 + len(queries)),
            jax.ShapeDtypeStruct((rows, 2 * cols + (0 if at else pair_cols)), BF),
            VMEM,
            [],
            8 * MIB,
            2 * rows * features * cols,
            2 * features * cols,
        )
        return swap(block, "wide", wide, 1)

    far = [far_swap(at) for at in range(most)]
    sums, pair = [], None
    for at in range(most):
        near = project(near_blocks[at])
        added, *rest = call(
            add_next_kernel if sums else add_first_kernel,
            (near, far[at], pair) if sums else (near, kv, far[at]),
            [VMEM] * 3,
            [full] if sums else [full, jax.ShapeDtypeStruct((rows, pair_cols), BF)],
            [VMEM] * (1 if sums else 2),
            [],
            2 * MIB,
            rows * 1024,
            rows * 4096,
        )
        pair = rest[0] if rest else pair
        sums.append(added)
    received = [swap(part, "wide", wide, d) for part, d in zip(sums, near_blocks)]
    far_last = far_swap(most)
    later, _ = lax.optimization_barrier((pieces, sums[-1]))
    near_last = project(near_blocks[most], later)
    turned = call(
        turn_kernel,
        later[:narrow],
        [VMEM] * narrow,
        jax.ShapeDtypeStruct((features, rows), BF),
        VMEM,
        [],
        2 * MIB,
        0,
        4 * rows * features,
    )
    near_last, turned = lax.optimization_barrier((near_last, turned))
    own = call(
        functools.partial(attend_kernel, narrow),
        (near_last, far_last, pair, *received),
        [VMEM] * (3 + len(received)),
        full,
        VMEM,
        [],
        4 * MIB,
        24 * rows * rows * cols,
        2 * rows * wide * full.shape[1],
    )
    width = 2 * cols
    sum_shapes = [jax.ShapeDtypeStruct((rows, features), F32)] * 2
    grad_shapes = [jax.ShapeDtypeStruct(w.shape, BF) for w in (w_query, w_output)]

    def grad_scratch(blocks):
        return [pltpu.VMEM((len(blocks), features, cols), BF), pltpu.VMEM((len(blocks), cols, features), BF), sems]

    def block_terms(distances, before=(), more=(), written=()):
        blocks = [(i, 0, d) for i, d in enumerate(distances)]
        parts = [*[same[d] for d in distances], *more]
        ins = (turned, *grad_pieces, *parts, w_query, w_output, *before)
        return call(
            functools.partial(block_kernel, blocks, list(written), cols, narrow, len(parts), bool(before)),
            ins,
            [VMEM] * (3 + narrow + len(parts)) + ([VMEM] * 2 + [ANY] * 2 if before else []),
            grad_shapes + sum_shapes,
            [ANY] * 2 + [VMEM] * 2,
            grad_scratch([*blocks, *written]),
            20 * MIB,
            8 * rows * features * cols * len(blocks),
            8 * features * cols * len(blocks),
            {len(ins) - 2: 0, len(ins) - 1: 1} if before else {},
        )

    same = {0: own, **{d: swap(own, "wide", wide, d) for d in near_blocks[:-1]}}
    first, rest = near_blocks[-2], near_blocks[:-2]
    groups = ([0, first], rest)
    joined = []
    for group in groups:
        if joined:
            *grads, out_sum, grad_sum = block_terms([0, first])
            same[rest[-1]], grads, out_sum, grad_sum = lax.optimization_barrier((same[rest[-1]], grads, out_sum, grad_sum))
        together = call(
            functools.partial(join_kernel, width),
            [same[d] for d in group],
            [VMEM] * len(group),
            jax.ShapeDtypeStruct((rows, width * len(group) + pair_cols), BF),
            VMEM,
            [],
            2 * MIB,
            0,
            4 * rows * full.shape[1] * len(group),
        )
        joined.append(swap(together, "wide", wide, 1))
    blocks = [[(i, width * at, d + 1) for at, d in enumerate(group)] for i, group in enumerate(groups)]
    written = [(len(rest), *blocks[0][0][1:])]
    *grads, out_sum, grad_sum = block_terms(rest, (out_sum, grad_sum, *grads), [joined[0]], written)
    out_sum, grad_sum = call(
        functools.partial(back_kernel, blocks[0], cols, 1),
        (joined[0], w_query, w_output, out_sum, grad_sum),
        [VMEM] * 5,
        sum_shapes,
        [VMEM] * 2,
        [],
        8 * MIB,
        4 * rows * features * cols * len(blocks[0]),
        4 * features * cols * len(blocks[0]),
    )
    parts = [*joined, *same.values()]
    piece_half = jax.ShapeDtypeStruct((narrow * piece, features), BF)
    piece_pair = jax.ShapeDtypeStruct((2 * piece, features), BF)
    near, far = call(
        functools.partial(back_last_kernel, blocks[1], cols, len(parts), piece),
        (*parts, w_query, w_output, wkv, out_sum, grad_sum),
        [VMEM] * (len(parts) + 5),
        [piece_half] * 2,
        [VMEM] * 2,
        [pltpu.VMEM((rows, features), F32), pltpu.VMEM((rows, features), F32)],
        8 * MIB,
        rows * weight_size,
        weight_size,
    )
    far = swap(far, "narrow", narrow, 1)
    sums = call(
        add_pieces_kernel,
        (near, far),
        [VMEM] * 2,
        [piece_pair] * (narrow // 2),
        [VMEM] * (narrow // 2),
        [],
        2 * MIB,
        2 * rows * features,
        12 * rows * features,
    )
    sums = [sums[0]] + [swap(sums[i], "narrow", narrow, 2 * i) for i in range(1, narrow // 2)]
    blocks = blocks[0][1:] + blocks[1]
    ins = (turned, *grad_pieces, *parts, *grads)
    grad_wq, grad_wo, grad_wkv = call(
        functools.partial(weight_grad_kernel, blocks, cols, narrow, len(parts)),
        ins,
        [VMEM] * (1 + narrow + len(parts)) + [ANY] * 2,
        grad_shapes + [jax.ShapeDtypeStruct(w_keyval.shape, BF)],
        [ANY] * 3,
        [pltpu.VMEM(w_keyval.shape, BF)] + grad_scratch(blocks),
        20 * MIB,
        8 * rows * features * cols * len(blocks),
        8 * features * cols * len(blocks),
        {len(ins) - 2: 0, len(ins) - 1: 1},
    )
    output, grad_tokens = call(
        finish_kernel,
        sums,
        [VMEM] * len(sums),
        [piece_shape] * 2,
        [VMEM] * 2,
        [],
        4 * MIB,
        2 * narrow * piece * features,
        4 * narrow * piece * features,
    )
    return (output, grad_tokens, grad_wq, grad_wkv, grad_wo)


def solution(mesh):
    return jax.shard_map(
        functools.partial(shards, mesh.shape["narrow"], mesh.shape["wide"]),
        mesh=mesh,
        in_specs=(
            P("narrow", "wide"),
            P("wide", "narrow"),
            P("wide", "narrow"),
            P("narrow", "wide"),
            P("narrow", "wide"),
        ),
        out_specs=(
            P("narrow", "wide"),
            P("narrow", "wide"),
            P("wide", "narrow"),
            P("wide", "narrow"),
            P("narrow", "wide"),
        ),
        check_vma=False,
    )
```
